128 devices in a mesh: ctx: 16 (over x, y), tp: 8 (over z, core).
Axes of the slice: x: 4, y: 4, z: 4, core: 2. Of those that a mesh axis runs over, the one named last changes fastest.
Arguments:
- queries: bfloat16 [4096, 8192], P('ctx', 'tp'), may hold values from -16 to 16
- keys: bfloat16 [4096, 1024], P('ctx', 'tp'), may hold values from -4 to 4
- values: bfloat16 [4096, 1024], P('ctx', 'tp'), may hold values from -6 to 6
- out_weight: bfloat16 [8192, 8192], P('tp'), may hold values from -0.09375 to 0.09375
- ssm_input: bfloat16 [4096, 16384], P('ctx', 'tp'), may hold values from -6 to 6
- ssm_gate: bfloat16 [4096, 16384], P('ctx', 'tp'), may hold values from -6 to 6
- in_map: bfloat16 [4096, 1024], P('ctx', 'tp'), may hold values from -0.1796875 to 0.1796875
- out_map: bfloat16 [4096, 1024], P('ctx', 'tp'), may hold values from -1.796875 to 1.796875
- log_decay: float32 [4096, 256], P('ctx', 'tp'), may hold values from -1 to 0
- skip: float32 [256], P('tp'), may hold values from 0.5 to 1.5
- norm_gain: float32 [16384], P('tp'), may hold values from 0.1 to 1.9
Outputs:
- mixed: bfloat16 [4096, 8192], P('ctx', 'tp')
- ssm_out: bfloat16 [4096, 16384], P('ctx', 'tp')
The draws below stay inside these ranges and needn't reach their ends.
All inputs are finite; a program needn't handle non-finite values.
Results may differ from the reference program's by a relative error of at most 0.019.
Values may be sent and summed in bfloat16 or wider, within the bound.
A program may use at most 128 MiB of HBM per device.

```python
import math
import jax
import jax.numpy as jnp
from jax import lax

D = 8192
HQ = 64
KVH = 8
HD = 128
MIXER_HEADS = 256
HP = 64
NS = 128
G = 8
BL = 128
TOK = 256
SEQUENCE_TOKENS = 4096
N_TP = 8


def draw_queries(key, part):
    key = jax.random.fold_in(key, 11)
    per_head = HQ // KVH
    base = jnp.clip(jax.random.normal(key, (SEQUENCE_TOKENS, KVH, per_head, HD)), -4.0, 4.0)
    return base.reshape(SEQUENCE_TOKENS, HQ * HD).astype(jnp.bfloat16)


def draw_keys(key, part):
    key = jax.random.fold_in(key, 12)
    base = jnp.clip(jax.random.normal(key, (SEQUENCE_TOKENS, KVH, HD)), -4.0, 4.0)
    return base.reshape(SEQUENCE_TOKENS, KVH * HD).astype(jnp.bfloat16)


def draw_log_decay(key, part):
    key = jax.random.fold_in(key, 31)
    random_subkeys = jax.random.split(key, 7)
    fast_share = 0.5
    coarse_estimate = jax.random.uniform(random_subkeys[1], (SEQUENCE_TOKENS, MIXER_HEADS), minval=0.5, maxval=1.5)
    fast_heads = jax.random.bernoulli(random_subkeys[0], fast_share, (MIXER_HEADS,))
    slow_rate = jnp.exp(jax.random.uniform(random_subkeys[2], (MIXER_HEADS,), minval=math.log(0.03), maxval=math.log(0.3))) / SEQUENCE_TOKENS
    fast_rate = jnp.exp(jax.random.uniform(random_subkeys[3], (MIXER_HEADS,), minval=math.log(1.0 / 50.0), maxval=math.log(1.0 / 30.0)))
    head_fraction = jnp.where(fast_heads, fast_rate, slow_rate)
    scatter_range = jax.random.uniform(random_subkeys[4], (SEQUENCE_TOKENS // TOK, MIXER_HEADS), minval=0.5, maxval=2.0)
    scatter_range = jnp.repeat(scatter_range, TOK, axis=0)
    spike_position = jax.random.randint(random_subkeys[5], (2,), 0, SEQUENCE_TOKENS)
    spike_length = jax.random.uniform(random_subkeys[6], (2, MIXER_HEADS), minval=0.22, maxval=0.5)
    match_count = lax.iota(jnp.int32, SEQUENCE_TOKENS)[:, None] == spike_position[None, :]
    spike_run = jnp.sum(jnp.where(match_count[:, :, None], spike_length[None], 0.0), axis=1)
    return (-(head_fraction[None, :] * coarse_estimate * scatter_range) - spike_run).astype(jnp.float32)


def spiked(values, key, source, target, shards_of, factor):
    def block_of(axis_at):
        return (jnp.arange(values.shape[axis_at]) // (values.shape[axis_at] // shards_of)).reshape((-1,) + (1,) * (values.ndim - 1 - axis_at))

    one_side = jax.random.permutation(key, shards_of)[block_of(target)]
    far = (block_of(target) + shards_of // 2) % shards_of
    return jnp.where((block_of(source) == one_side) | (block_of(source) == far), factor * values, values)


def block_levels(rng, extent, pieces, smallest, high):
    def one(position, blocks):
        draws = jax.random.uniform(jax.random.fold_in(jax.random.fold_in(rng, 6), position), (blocks,), jnp.float32, smallest / len(pieces), high / len(pieces))
        return jnp.repeat(jnp.exp(draws), extent[position] // blocks).reshape((-1,) + (1,) * (len(extent) - position - 1))

    gain = one(*pieces[0])
    for cut in pieces[1:]:
        gain = gain * one(*cut)
    return gain


def centred(stream_key, shape, spread, most, cuts=(), kind=jnp.bfloat16):
    factor_of = block_levels(stream_key, shape, cuts, -0.22, 0.18) if cuts else 1.0
    drawn = jax.random.normal(stream_key, shape, jnp.float32) * spread * factor_of
    return jnp.minimum(jnp.maximum(drawn, -most), most).astype(kind)


def bell_draw_with(rng, dims, width, reach, cuts, heavy, held_as=jnp.bfloat16):
    values = width * jax.random.normal(rng, dims, jnp.float32)
    if cuts:
        values = values * block_levels(rng, dims, cuts, -0.22, 0.18)
    return jnp.clip(spiked(values, jax.random.fold_in(rng, 3), *heavy), -reach, reach).astype(held_as)


def setup_inputs(seed: int = 0) -> dict:
    key_of = jax.random.split(jax.random.key(seed), 12)
    return {
        "queries": draw_queries(jax.random.fold_in(key_of[11], 71), 0),
        "keys": draw_keys(jax.random.fold_in(key_of[11], 71), 0),
        "values": centred(key_of[2], (SEQUENCE_TOKENS, KVH * HD), 1.0, 6.0, ((0, 16), (1, 8))),
        "out_weight": bell_draw_with(key_of[3], (HQ * HD, D), (HQ * HD) ** -0.5, 0.09375, ((0, 8),), (0, 1, 8, 2.0)),
        "ssm_input": centred(key_of[4], (SEQUENCE_TOKENS, MIXER_HEADS * HP), 1.0, 6.0, ((0, 16), (1, 8))),
        "ssm_gate": centred(key_of[5], (SEQUENCE_TOKENS, MIXER_HEADS * HP), 1.0, 6.0, ((0, 16), (1, 8))),
        "in_map": centred(key_of[6], (SEQUENCE_TOKENS, G * NS), 0.03, 0.1796875, ((0, 16), (1, 8))),
        "out_map": centred(key_of[7], (SEQUENCE_TOKENS, G * NS), 0.3, 1.796875, ((0, 16), (1, 8))),
        "log_decay": draw_log_decay(jax.random.fold_in(key_of[11], 71), 0),
        "skip": jnp.clip(0.5 + 1.0 * jax.random.uniform(key_of[9], (MIXER_HEADS,), jnp.float32) ** block_levels(key_of[9], (MIXER_HEADS,), ((0, 8),), -0.2, 0.2), 0.5, 1.5),
        "norm_gain": jnp.clip(1.0 + 0.18 * jax.random.normal(key_of[10], (MIXER_HEADS * HP,), jnp.float32), 0.1, 1.9),
    }


def attention_block(queries, keys, values, first_row, block_rows):
    per_head = HQ // KVH
    query_rows = lax.dynamic_slice_in_dim(queries, first_row, block_rows, 0)
    query_rows = query_rows.reshape(block_rows, KVH, per_head, HD).astype(jnp.float32)
    key_all = keys.reshape(SEQUENCE_TOKENS, KVH, HD).astype(jnp.float32)
    value_all = values.reshape(SEQUENCE_TOKENS, KVH, HD).astype(jnp.float32)
    query_pos = first_row + lax.iota(jnp.int32, block_rows)
    key_pos = lax.iota(jnp.int32, SEQUENCE_TOKENS)
    visible = key_pos[None, :] <= query_pos[:, None]

    def one_head(head_group):
        query_part = lax.dynamic_index_in_dim(query_rows, head_group, 1, keepdims=False)
        key_part = lax.dynamic_index_in_dim(key_all, head_group, 1, keepdims=False)
        value_part = lax.dynamic_index_in_dim(value_all, head_group, 1, keepdims=False)
        scores = jnp.einsum('tkd,sd->kts', query_part, key_part) / math.sqrt(HD)
        scores = jnp.where(visible[None], scores, -jnp.inf)
        top_score = lax.optimization_barrier(jnp.max(scores, axis=-1, keepdims=True))
        weights = jnp.exp(scores - top_score)
        total = lax.optimization_barrier(jnp.sum(weights, axis=-1, keepdims=True))
        rounded = lax.optimization_barrier(weights.astype(jnp.bfloat16)).astype(jnp.float32)
        return jnp.einsum('kts,sd->ktd', rounded, value_part) / total
    heads_out = lax.map(one_head, jnp.arange(KVH, dtype=jnp.int32))
    return heads_out.transpose(2, 0, 1, 3).reshape(block_rows, HQ * HD).astype(jnp.bfloat16)

def ssm_reference(ssm_input, ssm_gate, in_map, out_map, log_decay, skip, norm_gain):
    block_count = SEQUENCE_TOKENS // BL
    group_heads = MIXER_HEADS // G
    items = (ssm_input.reshape(block_count, BL, G, group_heads, HP), in_map.reshape(block_count, BL, G, NS), out_map.reshape(block_count, BL, G, NS), log_decay.reshape(block_count, BL, G, group_heads))
    skip_heads = skip.reshape(G, group_heads)
    causal = lax.iota(jnp.int32, BL)[:, None] >= lax.iota(jnp.int32, BL)[None, :]

    def block_step(carry_state, block_item):
        inputs, input_maps, output_maps, decays = block_item
        inputs_wide = inputs.astype(jnp.float32)
        in_wide = input_maps.astype(jnp.float32)
        out_wide = output_maps.astype(jnp.float32)
        within = jnp.cumsum(decays, axis=0)
        pair_maps = jnp.einsum('ign,jgn->gij', out_wide, in_wide)
        ordered = within.transpose(1, 2, 0)
        gap_logs = jnp.where(causal, ordered[..., :, None] - ordered[..., None, :], 0.0)
        mixing = jnp.where(causal, pair_maps[:, None] * jnp.exp(gap_logs), 0.0)
        mixing = lax.optimization_barrier(mixing.astype(jnp.bfloat16)).astype(jnp.float32)
        inner_part = jnp.einsum('gkij,jgkp->igkp', mixing, inputs_wide)
        carried_out = jnp.einsum('ign,gkpn->igkp', out_wide, carry_state, precision=lax.Precision.HIGHEST)
        block_y = inner_part + jnp.exp(within)[..., None] * carried_out + skip_heads[:, :, None] * inputs_wide
        remaining = jnp.exp(within[-1:] - within)
        carried = lax.optimization_barrier((inputs_wide * remaining[..., None]).astype(jnp.bfloat16)).astype(jnp.float32)
        block_state = jnp.einsum('jgkp,jgn->gkpn', carried, in_wide)
        next_state = jnp.exp(within[-1])[..., None, None] * carry_state + block_state
        return (next_state, block_y)
    initial = jnp.zeros((G, group_heads, HP, NS), jnp.float32)
    _, outputs = lax.scan(block_step, initial, items)
    ssm_y = outputs.reshape(SEQUENCE_TOKENS, G, group_heads * HP)
    gate_wide = ssm_gate.astype(jnp.float32).reshape(SEQUENCE_TOKENS, G, group_heads * HP)
    gated = ssm_y * jax.nn.silu(gate_wide)
    normed = gated * lax.rsqrt(lax.optimization_barrier(jnp.mean(gated * gated, axis=-1, keepdims=True)) + 1e-05)
    normed = normed * norm_gain.reshape(G, group_heads * HP)
    return normed.reshape(SEQUENCE_TOKENS, MIXER_HEADS * HP).astype(jnp.bfloat16)

def reference(queries, keys, values, out_weight, ssm_input, ssm_gate, in_map, out_map, log_decay, skip, norm_gain):
    block_rows = math.gcd(SEQUENCE_TOKENS, 512)
    starts = jnp.arange(SEQUENCE_TOKENS // block_rows, dtype=jnp.int32) * block_rows
    blocks = lax.map(lambda first_row: attention_block(queries, keys, values, first_row, block_rows), starts)
    attention = blocks.reshape(SEQUENCE_TOKENS, HQ * HD)
    column_width = HQ * HD // N_TP
    summed = jnp.zeros((SEQUENCE_TOKENS, D), jnp.float32)
    for shard_number in range(N_TP):
        low_col = shard_number * column_width
        partial_sum = jnp.dot(attention[:, low_col:low_col + column_width], out_weight[low_col:low_col + column_width], preferred_element_type=jnp.float32)
        summed = summed + lax.optimization_barrier(partial_sum.astype(jnp.bfloat16)).astype(jnp.float32)
    mixed = summed.astype(jnp.bfloat16)
    ssm_out = ssm_reference(ssm_input, ssm_gate, in_map, out_map, log_decay, skip, norm_gain)
    return (mixed, ssm_out)
```

```python
import math

import jax
import jax.numpy as jnp
from jax import lax
from jax.experimental import pallas as pl
from jax.experimental.pallas import tpu as pltpu
from jax.sharding import PartitionSpec as P

HD = 128
HP = 64
NS = 128
BL = 128
SIDE = 4
RANKS = SIDE * SIDE
HEADS = 8
MIXERS = 32
TOK = 256
HALF = 128
WIDE = 1024
FEATURES = MIXERS * HP
PIECE = NS + 16
MESH = pl.DeviceIdType.MESH
F32 = jnp.float32
BF16 = jnp.bfloat16
SCORE_SCALE = math.log2(math.e) / math.sqrt(HD)


def dot(a, b):
    return lax.dot_general(a, b, (((1,), (0,)), ((), ())), preferred_element_type=F32)


def dot_t(a, b):
    return lax.dot_general(a, b, (((1,), (1,)), ((), ())), preferred_element_type=F32)


def iota(shape, dim):
    return lax.broadcasted_iota(jnp.int32, shape, dim)


def split3(v):
    hi = v.astype(BF16)
    rest = v - hi.astype(F32)
    mid = rest.astype(BF16)
    lo = (rest - mid.astype(F32)).astype(BF16)
    return hi, mid, lo


def lane_split(v):
    hi, mid, lo = split3(v)
    group = iota(v.shape, 1) // MIXERS
    parts = jnp.where(
        group == 0,
        hi.astype(F32),
        jnp.where(group == 1, mid.astype(F32), jnp.where(group == 2, lo.astype(F32), 0.0)),
    )
    return parts.astype(BF16)


def spread(first_head, lanes_per_head):
    return (
        iota((128, 256), 0) % MIXERS == first_head + iota((128, 256), 1) // lanes_per_head
    ).astype(F32).astype(BF16)


def kernel(
    q_hbm, k_hbm, v_hbm, w_hbm, x_hbm, g_hbm, b_hbm, c_hbm, ld_hbm, skip_hbm, gain_hbm,
    mixed_hbm, ssm_hbm,
    qv, kv, wv, xv, gv, bv, cv, ldv, skv, gnv,
    cumsplit, cum_rows, pair_maps, bt, remsplit, expsplit, expx, skx, inner, s0buf,
    st_send, st_recv, in_send, in_recv, ssm_v,
    acc, top, att, own, xs, xr, fs, fr, ns, nr, mixed_v,
    load_sem, kv_send, kv_recv, sts, str_, ins, inr, xss, xsr, fss, fsr, nss, nsr, out_sem,
):
    rank = lax.axis_index("ctx")
    tp = lax.axis_index("tp")
    x, y = rank // SIDE, rank % SIDE
    z, core = tp // 2, tp % 2
    up = 2 * ((z + 1) % SIDE) + core
    down = 2 * ((z + SIDE - 1) % SIDE) + core
    partner = 2 * z + 1 - core

    loads = [
        (k_hbm, kv.at[rank, 0]),
        (v_hbm, kv.at[rank, 1]),
        (ld_hbm, ldv),
        (skip_hbm, skv),
        (x_hbm, xv),
        (b_hbm, bv),
        (c_hbm, cv),
        (q_hbm, qv),
        (w_hbm, wv),
        (g_hbm, gv),
        (gain_hbm, gnv),
    ]
    copies = [pltpu.make_async_copy(a, b, load_sem.at[i]) for i, (a, b) in enumerate(loads)]
    for copy in copies:
        copy.start()

    barrier = pltpu.get_barrier_semaphore()

    def greet(d, _):
        pl.semaphore_signal(barrier, inc=1, device_id=((rank + d) % RANKS, tp), device_id_type=MESH)
        return 0

    lax.fori_loop(1, RANKS, greet, 0)
    for other in (partner, up, down):
        pl.semaphore_signal(barrier, inc=1, device_id=(rank, other), device_id_type=MESH)
    pl.semaphore_wait(barrier, RANKS - 1 + 3)

    def kv_copy(block, dest, sem):
        return pltpu.make_async_remote_copy(
            src_ref=kv.at[block],
            dst_ref=kv.at[block],
            send_sem=kv_send.at[sem],
            recv_sem=kv_recv.at[block],
            device_id=(dest, tp),
            device_id_type=MESH,
        )

    copies[0].wait()
    copies[1].wait()
    for d in range(1, SIDE):
        kv_copy(rank, SIDE * x + (y + d) % SIDE, d - 1).start()
    for xd in range(1, SIDE):

        @pl.when((core == 1) & (xd > x))
        def _():
            kv_copy(rank, SIDE * xd + y, 2 + xd).start()

    copies[2].wait()
    copies[3].wait()
    repeat = (iota((MIXERS, 128), 1) % MIXERS == iota((MIXERS, 128), 0)).astype(F32).astype(BF16)
    lower = (iota((BL, BL), 0) >= iota((BL, BL), 1)).astype(F32).astype(BF16)
    decays = [dot(part, repeat) for part in split3(ldv[...])]
    decays = (decays[0] + decays[1]) + decays[2]
    for b in range(2):
        rows = slice(b * BL, (b + 1) * BL)
        cum = [dot(lower, part) for part in split3(decays[rows])]
        cum = (cum[0] + cum[1]) + cum[2]
        cumsplit[rows, :] = lane_split(cum)
        cum_rows[b] = cum.T
        expsplit[rows, :] = lane_split(jnp.exp(cum))
        remsplit[rows, :] = lane_split(jnp.exp(cum[BL - 1 : BL] - cum))
    skips = [dot(part, repeat) for part in split3(jnp.broadcast_to(skv[...], (8, MIXERS)))]
    skip_split = lane_split((skips[0] + skips[1]) + skips[2])
    copies[4].wait()
    copies[5].wait()
    for b in range(2):
        bt[b] = bv[b * BL : (b + 1) * BL, :].astype(F32).T.astype(BF16)

    def state_chunk(ci, _):
        cols = pl.ds(pl.multiple_of(ci * 256, 256), 256)
        e = spread(4 * ci, HP)
        ex = dot(expsplit[...], e)
        expx[:, cols] = ex
        skx[:, cols] = dot(skip_split, e)
        carried = (xv[:, cols].astype(F32) * dot(remsplit[...], e)).astype(BF16)
        s0 = dot(bt[0], carried[:BL])
        s1 = dot(bt[1], carried[BL:])
        s0buf[:, cols] = s0
        d0, d1 = ex[BL - 1 : BL], ex[2 * BL - 1 :]
        end = (d1 * s0 + s1).astype(BF16)
        decay = d0 * d1
        hi = decay.astype(BF16).astype(F32)
        row = iota((16, 256), 0)
        tail = jnp.where(row == 0, hi, jnp.where(row == 1, decay - hi, 0.0)).astype(BF16)
        for u in range(2):
            st_send[2 * ci + u, :NS, :] = end[:, u * 128 : (u + 1) * 128]
            st_send[2 * ci + u, NS:, :] = tail[:, u * 128 : (u + 1) * 128]
        return 0

    lax.fori_loop(0, FEATURES // 256, state_chunk, 0)

    def state_copy(piece):
        return pltpu.make_async_remote_copy(
            src_ref=st_send.at[piece],
            dst_ref=st_recv.at[rank],
            send_sem=sts.at[piece],
            recv_sem=str_.at[rank],
            device_id=(piece, tp),
            device_id_type=MESH,
        )

    def send_state(d, _):
        state_copy((rank + d) % RANKS).start()
        return 0

    lax.fori_loop(1, RANKS, send_state, 0)
    st_recv[rank] = st_send[rank]

    for d in range(1, SIDE):
        kv_copy(SIDE * x + (y + d) % SIDE, rank, 0).wait_recv()
    for xd in range(1, SIDE):
        for yb in range(SIDE):

            @pl.when((core == 0) & (xd > x))
            def _():
                kv_copy(SIDE * x + yb, SIDE * xd + y, 3 + 4 * (xd - 1) + yb).start()

    for xb in range(SIDE - 1):

        @pl.when((core == 1) & (xb < x))
        def _():
            kv_copy(SIDE * xb + y, rank, 0).wait_recv()
            for d in range(1, SIDE):
                kv_copy(SIDE * xb + y, SIDE * x + (y + d) % SIDE, 6 + 3 * xb + d - 1).start()

    copies[6].wait()
    for b in range(2):
        rows = slice(b * BL, (b + 1) * BL)
        maps = dot_t(cv[rows, :], bv[rows, :])
        pair_maps[b] = jnp.where(iota((BL, BL), 0) >= iota((BL, BL), 1), maps, 0.0)
    low_lanes = (iota((BL, 128), 1) < HP).astype(F32).astype(BF16)
    high_lanes = (iota((BL, 128), 1) >= HP).astype(F32).astype(BF16)

    def inner_pair(p, _):
        cols = pl.ds(pl.multiple_of(p * 128, 128), 128)
        down_col = dot(cumsplit[...], spread(2 * p, 128))
        for b in range(2):
            rows = slice(b * BL, (b + 1) * BL)
            mixing = []
            for u in range(2):
                gap = down_col[rows, u * 128 : (u + 1) * 128] - cum_rows[b, pl.ds(2 * p + u, 1), :]
                mixing.append((pair_maps[b] * jnp.exp(jnp.minimum(gap, 0.0))).astype(BF16))
            xp = xv[rows, cols]
            both = jnp.concatenate([xp * low_lanes, xp * high_lanes], axis=0)
            inner[rows, cols] = dot(jnp.concatenate(mixing, axis=1), both)
        return 0

    lax.fori_loop(0, MIXERS // 2, inner_pair, 0)

    def in_copy(dest):
        return pltpu.make_async_remote_copy(
            src_ref=in_send.at[dest],
            dst_ref=in_recv.at[rank],
            send_sem=ins.at[dest],
            recv_sem=inr.at[rank],
            device_id=(dest, tp),
            device_id_type=MESH,
        )

    def prefix(i, before):
        @pl.when(i != rank)
        def _():
            pltpu.make_async_copy(st_recv.at[i], st_recv.at[i], str_.at[i]).wait()

        in_send[i] = before.astype(BF16)

        @pl.when(i != rank)
        def _():
            in_copy(i).start()

        tail = st_recv[i, NS:, :].astype(F32)
        return (tail[0:1] + tail[1:2]) * before + st_recv[i, :NS, :].astype(F32)

    lax.fori_loop(0, RANKS, prefix, jnp.zeros((NS, 128), F32))
    in_recv[rank] = in_send[rank]

    copies[7].wait()
    ones = jnp.ones((WIDE, HD), BF16)

    def absorb(half, row_index, first):
        def pair(hp, _):
            for u in range(2):
                h = 2 * hp + u
                q = qv[half * HALF : (half + 1) * HALF, pl.ds(pl.multiple_of(h * HD, HD), HD)]
                keys = kv[pl.ds(SIDE * row_index, SIDE), 0].reshape(WIDE, HD)
                values = kv[pl.ds(SIDE * row_index, SIDE), 1].reshape(WIDE, HD)
                values = jnp.concatenate([values, ones], axis=1)
                scores = dot_t(q, keys)
                if first:
                    place = iota((HALF, WIDE), 0) + (y * TOK + half * HALF)
                    scores = jnp.where(iota((HALF, WIDE), 1) <= place, scores, -1e30)
                    new = jnp.max(scores, axis=1, keepdims=True)
                else:
                    old = top[h, :, 0:1]
                    new = jnp.maximum(old, jnp.max(scores, axis=1, keepdims=True))
                weights = jnp.exp2(scores * SCORE_SCALE - new * SCORE_SCALE).astype(BF16)
                add = dot(weights, values)
                if first:
                    acc[h] = add
                else:
                    acc[h] = acc[h] * jnp.exp2((old - new) * SCORE_SCALE) + add
                top[h] = jnp.broadcast_to(new, (HALF, 128))
            return 0

        lax.fori_loop(0, HEADS // 2, pair, 0)

    def wait_row(row_index):
        for yb in range(SIDE):

            @pl.when((core == 0) | (yb != y))
            def _():
                kv_copy(SIDE * row_index + yb, rank, 0).wait_recv()

    def finish(half):
        def one(h, _):
            a = acc[h]
            att[:, pl.ds(pl.multiple_of(h * HD, HD), HD)] = (a[:, :HD] / a[:, HD:]).astype(BF16)
            return 0

        lax.fori_loop(0, HEADS, one, 0)

    def project(block):
        cols = pl.ds(pl.multiple_of(block * WIDE, WIDE), WIDE)
        return dot(att[...], wv[:, cols])

    def far_first(i):
        return (2 + i) % SIDE

    def xs_copy(half, d):
        return pltpu.make_async_remote_copy(
            src_ref=xs.at[half, d],
            dst_ref=xr.at[half, d],
            send_sem=xss.at[half, d],
            recv_sem=xsr.at[half, d],
            device_id=(rank, partner),
            device_id_type=MESH,
        )

    def ring_copy(src, dst, send, recv, half, way):
        return pltpu.make_async_remote_copy(
            src_ref=src.at[half, way],
            dst_ref=dst.at[half, way],
            send_sem=send.at[half, way],
            recv_sem=recv.at[half, way],
            device_id=(rank, up if way == 0 else down),
            device_id_type=MESH,
        )

    def far_copy(half, way):
        return ring_copy(fs, fr, fss, fsr, half, way)

    def near_copy(half, way):
        return ring_copy(ns, nr, nss, nsr, half, way)

    STEP = 32

    def project_and_send(half):
        def for_partner(i, _):
            d = far_first(i)
            xs[half, d] = project(2 * ((z + d) % SIDE) + 1 - core).astype(BF16)
            xs_copy(half, d).start()
            return 0

        def for_own(i, _):
            d = far_first(i)
            own[half, d] = project(2 * ((z + d) % SIDE) + core)
            return 0

        lax.fori_loop(0, SIDE, for_partner, 0)
        for_own(0, 0)
        xs_copy(half, 2).wait_recv()
        for way in range(2):

            def far_sum(t, _):
                rows = pl.ds(pl.multiple_of(64 * way + t * STEP, STEP), STEP)
                fs[half, way, pl.ds(pl.multiple_of(t * STEP, STEP), STEP), :] = (
                    own[half, 2, rows, :] + xr[half, 2, rows, :].astype(F32)
                ).astype(BF16)
                return 0

            lax.fori_loop(0, 64 // STEP, far_sum, 0)
            far_copy(half, way).start()
        lax.fori_loop(1, SIDE, for_own, 0)

    def near(half):
        for way in range(2):
            d = 1 if way == 0 else 3
            xs_copy(half, d).wait_recv()
            far_copy(half, way).wait_recv()

            def near_sum(t, _):
                for has_far in (True, False):
                    start = 64 * way if has_far else 64 - 64 * way
                    rows = pl.ds(pl.multiple_of(start + t * STEP, STEP), STEP)
                    total = own[half, d, rows, :] + xr[half, d, rows, :].astype(F32)
                    if has_far:
                        far = fr[half, way, pl.ds(pl.multiple_of(t * STEP, STEP), STEP), :]
                        total = total + far.astype(F32)
                    ns[half, way, rows, :] = total.astype(BF16)
                return 0

            lax.fori_loop(0, 64 // STEP, near_sum, 0)
            near_copy(half, way).start()

    def last(half):
        xs_copy(half, 0).wait_recv()
        near_copy(half, 0).wait_recv()
        near_copy(half, 1).wait_recv()

        def last_sum(t, _):
            rows = pl.ds(pl.multiple_of(t * STEP, STEP), STEP)
            total = own[half, 0, rows, :] + xr[half, 0, rows, :].astype(F32)
            total = total + nr[half, 0, rows, :].astype(F32) + nr[half, 1, rows, :].astype(F32)
            mixed_v[half, rows, :] = total.astype(BF16)
            return 0

        lax.fori_loop(0, HALF // STEP, last_sum, 0)
        mixed_out(half).start()

    def mixed_out(half):
        return pltpu.make_async_copy(
            mixed_v.at[half], mixed_hbm.at[half * HALF : (half + 1) * HALF], out_sem.at[half]
        )

    absorb(0, x, True)
    for i in range(1, SIDE):

        @pl.when(i <= x)
        def _():
            wait_row(x - i)
            absorb(0, x - i, False)

    finish(0)
    copies[8].wait()
    project_and_send(0)

    absorb(1, x, True)
    for i in range(1, SIDE):

        @pl.when(i <= x)
        def _():
            absorb(1, x - i, False)

        if i == 1:
            near(0)

    finish(1)
    project_and_send(1)

    copies[9].wait()
    copies[10].wait()

    def entered(i, _):
        @pl.when(i != rank)
        def _():
            pltpu.make_async_copy(in_recv.at[i], in_recv.at[i], inr.at[i]).wait()

        return 0

    lax.fori_loop(0, RANKS, entered, 0)

    def gate_chunk(ci, squares):
        cols = pl.ds(pl.multiple_of(ci * 256, 256), 256)
        enter = jnp.concatenate([in_recv[2 * ci], in_recv[2 * ci + 1]], axis=1)
        second = (expx[BL - 1 : BL, cols] * enter.astype(F32) + s0buf[:, cols]).astype(BF16)
        out = []
        for b, state in enumerate((enter, second)):
            rows = slice(b * BL, (b + 1) * BL)
            value = inner[rows, cols] + expx[rows, cols] * dot(cv[rows, :], state)
            value = value + skx[0:1, cols] * xv[rows, cols].astype(F32)
            gate = gv[rows, cols].astype(F32)
            value = value * (gate / (1.0 + jnp.exp(-gate)))
            inner[rows, cols] = value
            square = value * value
            out.append(squares[b] + (square[:, :128] + square[:, 128:]))
        return tuple(out)

    zero = jnp.zeros((BL, 128), F32)
    squares = lax.fori_loop(0, FEATURES // 256, gate_chunk, (zero, zero))
    factors = [
        lax.rsqrt(jnp.sum(s, axis=1, keepdims=True) * (1.0 / FEATURES) + 1e-05) for s in squares
    ]

    def norm_chunk(ci, _):
        cols = pl.ds(pl.multiple_of(ci * 256, 256), 256)
        for b in range(2):
            rows = slice(b * BL, (b + 1) * BL)
            ssm_v[rows, cols] = (inner[rows, cols] * factors[b] * gnv[:, cols]).astype(BF16)
        return 0

    lax.fori_loop(0, FEATURES // 256, norm_chunk, 0)
    ssm_out = pltpu.make_async_copy(ssm_v, ssm_hbm, out_sem.at[2])
    ssm_out.start()

    near(1)
    last(0)
    last(1)

    for d in range(1, SIDE):
        kv_copy(rank, rank, d - 1).wait_send()
    for xd in range(1, SIDE):

        @pl.when((core == 1) & (xd > x))
        def _():
            kv_copy(rank, rank, 2 + xd).wait_send()

        for yb in range(SIDE):

            @pl.when((core == 0) & (xd > x))
            def _():
                kv_copy(rank, rank, 3 + 4 * (xd - 1) + yb).wait_send()

    for xb in range(SIDE - 1):

        @pl.when((core == 1) & (xb < x))
        def _():
            for d in range(1, SIDE):
                kv_copy(rank, rank, 6 + 3 * xb + d - 1).wait_send()

    def states_left(d, _):
        other = (rank + d) % RANKS
        state_copy(other).wait_send()
        in_copy(other).wait_send()
        return 0

    lax.fori_loop(1, RANKS, states_left, 0)
    for half in range(2):
        for d in range(SIDE):
            xs_copy(half, d).wait_send()
        for way in range(2):
            far_copy(half, way).wait_send()
            near_copy(half, way).wait_send()
    ssm_out.wait()
    mixed_out(0).wait()
    mixed_out(1).wait()


def local(
    queries, keys, values, out_weight, ssm_input, ssm_gate, in_map, out_map, log_decay, skip, norm_gain
):
    anywhere = pl.BlockSpec(memory_space=pl.ANY)
    sem = pltpu.SemaphoreType.DMA
    scratch = [
        pltpu.VMEM((TOK, HEADS * HD), BF16),
        pltpu.VMEM((RANKS, 2, TOK, HD), BF16),
        pltpu.VMEM((HEADS * HD, 8 * WIDE), BF16),
        pltpu.VMEM((TOK, FEATURES), BF16),
        pltpu.VMEM((TOK, FEATURES), BF16),
        pltpu.VMEM((TOK, NS), BF16),
        pltpu.VMEM((TOK, NS), BF16),
        pltpu.VMEM((TOK, MIXERS), F32),
        pltpu.VMEM((1, MIXERS), F32),
        pltpu.VMEM((1, FEATURES), F32),
        pltpu.VMEM((TOK, 128), BF16),
        pltpu.VMEM((2, 128, BL), F32),
        pltpu.VMEM((2, BL, BL), F32),
        pltpu.VMEM((2, NS, BL), BF16),
        pltpu.VMEM((TOK, 128), BF16),
        pltpu.VMEM((TOK, 128), BF16),
        pltpu.VMEM((TOK, FEATURES), F32),
        pltpu.VMEM((8, FEATURES), F32),
        pltpu.VMEM((TOK, FEATURES), F32),
        pltpu.VMEM((NS, FEATURES), F32),
        pltpu.VMEM((RANKS, PIECE, 128), BF16),
        pltpu.VMEM((RANKS, PIECE, 128), BF16),
        pltpu.VMEM((RANKS, NS, 128), BF16),
        pltpu.VMEM((RANKS, NS, 128), BF16),
        pltpu.VMEM((TOK, FEATURES), BF16),
        pltpu.VMEM((HEADS, HALF, 2 * HD), F32),
        pltpu.VMEM((HEADS, HALF, 128), F32),
        pltpu.VMEM((HALF, HEADS * HD), BF16),
        pltpu.VMEM((2, SIDE, HALF, WIDE), F32),
        pltpu.VMEM((2, SIDE, HALF, WIDE), BF16),
        pltpu.VMEM((2, SIDE, HALF, WIDE), BF16),
        pltpu.VMEM((2, 2, HALF // 2, WIDE), BF16),
        pltpu.VMEM((2, 2, HALF // 2, WIDE), BF16),
        pltpu.VMEM((2, 2, HALF, WIDE), BF16),
        pltpu.VMEM((2, 2, HALF, WIDE), BF16),
        pltpu.VMEM((2, HALF, WIDE), BF16),
        sem((11,)),
        sem((16,)),
        sem((RANKS,)),
        sem((RANKS,)),
        sem((RANKS,)),
        sem((RANKS,)),
        sem((RANKS,)),
        sem((2, SIDE)),
        sem((2, SIDE)),
        sem((2, 2)),
        sem((2, 2)),
        sem((2, 2)),
        sem((2, 2)),
        sem((3,)),
    ]
    return pl.pallas_call(
        kernel,
        out_shape=(
            jax.ShapeDtypeStruct((TOK, WIDE), BF16),
            jax.ShapeDtypeStruct((TOK, FEATURES), BF16),
        ),
        in_specs=[anywhere] * 11,
        out_specs=(anywhere, anywhere),
        scratch_shapes=scratch,
        compiler_params=pltpu.CompilerParams(
            collective_id=0, has_side_effects=True, vmem_limit_bytes=60 * 1024 * 1024
        ),
        cost_estimate=pl.CostEstimate(
            flops=9_000_000_000, bytes_accessed=24_000_000, transcendentals=9_000_000
        ),
    )(
        queries, keys, values, out_weight, ssm_input, ssm_gate, in_map, out_map, log_decay,
        skip.reshape(1, MIXERS), norm_gain.reshape(1, FEATURES),
    )


def solution(mesh):
    in_specs = (
        P("ctx", "tp"),
        P("ctx", "tp"),
        P("ctx", "tp"),
        P("tp", None),
        P("ctx", "tp"),
        P("ctx", "tp"),
        P("ctx", "tp"),
        P("ctx", "tp"),
        P("ctx", "tp"),
        P("tp"),
        P("tp"),
    )
    out_specs = (P("ctx", "tp"), P("ctx", "tp"))
    return jax.shard_map(local, mesh=mesh, in_specs=in_specs, out_specs=out_specs, check_vma=False)
```

```python
import math

import jax
import jax.numpy as jnp
from jax import lax
from jax.experimental import pallas as pl
from jax.experimental.pallas import tpu as pltpu
from jax.sharding import PartitionSpec as P

HD = 128
HP = 64
NS = 128
BL = 128
SIDE = 4
RANKS = SIDE * SIDE
HEADS = 8
MIXERS = 32
TOK = 256
HALF = 128
WIDE = 1024
FEATURES = MIXERS * HP
PIECE = NS + 16
MESH = pl.DeviceIdType.MESH
F32 = jnp.float32
BF16 = jnp.bfloat16
SCORE_SCALE = math.log2(math.e) / math.sqrt(HD)


def dot(a, b):
    return lax.dot_general(a, b, (((1,), (0,)), ((), ())), preferred_element_type=F32)


def dot_t(a, b):
    return lax.dot_general(a, b, (((1,), (1,)), ((), ())), preferred_element_type=F32)


def iota(shape, dim):
    return lax.broadcasted_iota(jnp.int32, shape, dim)


def split3(v):
    hi = v.astype(BF16)
    rest = v - hi.astype(F32)
    mid = rest.astype(BF16)
    lo = (rest - mid.astype(F32)).astype(BF16)
    return hi, mid, lo


def lane_split(v):
    hi, mid, lo = split3(v)
    group = iota(v.shape, 1) // MIXERS
    parts = jnp.where(
        group == 0,
        hi.astype(F32),
        jnp.where(group == 1, mid.astype(F32), jnp.where(group == 2, lo.astype(F32), 0.0)),
    )
    return parts.astype(BF16)


def spread(first_head, lanes_per_head):
    return (
        iota((128, 256), 0) % MIXERS == first_head + iota((128, 256), 1) // lanes_per_head
    ).astype(F32).astype(BF16)


def kernel(
    q_hbm, k_hbm, v_hbm, w_hbm, x_hbm, g_hbm, b_hbm, c_hbm, ld_hbm, skip_hbm, gain_hbm,
    mixed_hbm, ssm_hbm,
    qv, kv, wv, xv, gv, bv, cv, ldv, skv, gnv,
    cumsplit, cum_rows, pair_maps, bt, remsplit, expsplit, expx, skx, inner, s0buf,
    st_send, st_recv, in_send, in_recv, ssm_v,
    acc, top, att, own, xs, xr, fs, fr, ns, nr, mixed_v,
    load_sem, kv_send, kv_recv, sts, str_, ins, inr, xss, xsr, fss, fsr, nss, nsr, out_sem,
):
    rank = lax.axis_index("ctx")
    tp = lax.axis_index("tp")
    x, y = rank // SIDE, rank % SIDE
    z, core = tp // 2, tp % 2
    up = 2 * ((z + 1) % SIDE) + core
    down = 2 * ((z + SIDE - 1) % SIDE) + core
    partner = 2 * z + 1 - core

    loads = [
        (k_hbm, kv.at[rank, 0]),
        (v_hbm, kv.at[rank, 1]),
        (ld_hbm, ldv),
        (skip_hbm, skv),
        (x_hbm, xv),
        (b_hbm, bv),
        (c_hbm, cv),
        (q_hbm, qv),
        (w_hbm, wv),
        (g_hbm, gv),
        (gain_hbm, gnv),
    ]
    copies = [pltpu.make_async_copy(a, b, load_sem.at[i]) for i, (a, b) in enumerate(loads)]
    for copy in copies:
        copy.start()

    barrier = pltpu.get_barrier_semaphore()

    def greet(d, _):
        pl.semaphore_signal(barrier, inc=1, device_id=((rank + d) % RANKS, tp), device_id_type=MESH)
        return 0

    lax.fori_loop(1, RANKS, greet, 0)
    for other in (partner, up, down):
        pl.semaphore_signal(barrier, inc=1, device_id=(rank, other), device_id_type=MESH)
    pl.semaphore_wait(barrier, RANKS - 1 + 3)

    def kv_copy(block, dest, sem):
        return pltpu.make_async_remote_copy(
            src_ref=kv.at[block],
            dst_ref=kv.at[block],
            send_sem=kv_send.at[sem],
            recv_sem=kv_recv.at[block],
            device_id=(dest, tp),
            device_id_type=MESH,
        )

    def row_needs(block_y, dest_y):
        return (dest_y > block_y) | ((core == 0) & (x < SIDE - 1))

    copies[0].wait()
    copies[1].wait()
    for xd in range(SIDE - 1, 0, -1):

        @pl.when(xd > x)
        def _():
            kv_copy(rank, SIDE * xd + y, 2 + xd).start()

    for d in range(1, SIDE):
        yd = (y + d) % SIDE

        @pl.when(row_needs(y, yd))
        def _():
            kv_copy(rank, SIDE * x + yd, d - 1).start()

    copies[2].wait()
    copies[3].wait()
    repeat = (iota((MIXERS, 128), 1) % MIXERS == iota((MIXERS, 128), 0)).astype(F32).astype(BF16)
    lower = (iota((BL, BL), 0) >= iota((BL, BL), 1)).astype(F32).astype(BF16)
    decays = jnp.concatenate([ldv[...]] * 4, axis=0)
    for b in range(2):
        rows = slice(b * BL, (b + 1) * BL)
        cum = [dot(lower, part) for part in split3(decays[:, rows].T)]
        cum = (cum[0] + cum[1]) + cum[2]
        cumsplit[rows, :] = lane_split(cum)
        cum_rows[b] = cum.T
        expsplit[rows, :] = lane_split(jnp.exp(cum))
        remsplit[rows, :] = lane_split(jnp.exp(cum[BL - 1 : BL] - cum))
    skips = [dot(part, repeat) for part in split3(jnp.broadcast_to(skv[...], (8, MIXERS)))]
    skip_split = lane_split((skips[0] + skips[1]) + skips[2])
    copies[4].wait()
    copies[5].wait()
    for b in range(2):
        bt[b] = bv[b * BL : (b + 1) * BL, :].astype(F32).T.astype(BF16)

    def state_chunk(ci, _):
        cols = pl.ds(pl.multiple_of(ci * 256, 256), 256)
        e = spread(4 * ci, HP)
        ex = dot(expsplit[...], e)
        expx[:, cols] = ex
        skx[:, cols] = dot(skip_split, e)
        carried = (xv[:, cols].astype(F32) * dot(remsplit[...], e)).astype(BF16)
        s0 = dot(bt[0], carried[:BL])
        s1 = dot(bt[1], carried[BL:])
        s0buf[:, cols] = s0
        d0, d1 = ex[BL - 1 : BL], ex[2 * BL - 1 :]
        end = (d1 * s0 + s1).astype(BF16)
        decay = d0 * d1
        hi = decay.astype(BF16).astype(F32)
        row = iota((16, 256), 0)
        tail = jnp.where(row == 0, hi, jnp.where(row == 1, decay - hi, 0.0)).astype(BF16)
        for u in range(2):
            st_send[2 * ci + u, :NS, :] = end[:, u * 128 : (u + 1) * 128]
            st_send[2 * ci + u, NS:, :] = tail[:, u * 128 : (u + 1) * 128]
        return 0

    lax.fori_loop(0, FEATURES // 256, state_chunk, 0)

    def state_copy(piece):
        return pltpu.make_async_remote_copy(
            src_ref=st_send.at[piece],
            dst_ref=st_recv.at[rank],
            send_sem=sts.at[piece],
            recv_sem=str_.at[rank],
            device_id=(piece, tp),
            device_id_type=MESH,
        )

    def send_state(d, _):
        state_copy((rank + d) % RANKS).start()
        return 0

    for d in range(1, SIDE):
        yb = (y + d) % SIDE

        @pl.when(row_needs(yb, y))
        def _():
            kv_copy(SIDE * x + yb, rank, 0).wait_recv()

        @pl.when(jnp.logical_not(row_needs(yb, y)))
        def _():
            kv[SIDE * x + yb, 1] = jnp.zeros((TOK, HD), BF16)

        for xd in range(SIDE - 1, 0, -1):

            @pl.when((core == 0) & (xd > x))
            def _():
                kv_copy(SIDE * x + yb, SIDE * xd + y, 6 + 3 * (xd - 1) + d - 1).start()

    for xb in range(SIDE - 2, -1, -1):

        @pl.when((core == 1) & (xb < x))
        def _():
            kv_copy(SIDE * xb + y, rank, 0).wait_recv()
            for d in range(1, SIDE):
                kv_copy(SIDE * xb + y, SIDE * x + (y + d) % SIDE, 6 + 3 * xb + d - 1).start()

    copies[6].wait()
    for b in range(2):
        rows = slice(b * BL, (b + 1) * BL)
        maps = dot_t(cv[rows, :], bv[rows, :])
        pair_maps[b] = jnp.where(iota((BL, BL), 0) >= iota((BL, BL), 1), maps, 0.0)
    low_lanes = (iota((BL, 128), 1) < HP).astype(F32).astype(BF16)
    high_lanes = (iota((BL, 128), 1) >= HP).astype(F32).astype(BF16)

    def inner_pair(p, _):
        cols = pl.ds(pl.multiple_of(p * 128, 128), 128)
        down_col = dot(cumsplit[...], spread(2 * p, 128))
        for b in range(2):
            rows = slice(b * BL, (b + 1) * BL)
            mixing = []
            for u in range(2):
                gap = down_col[rows, u * 128 : (u + 1) * 128] - cum_rows[b, pl.ds(2 * p + u, 1), :]
                mixing.append((pair_maps[b] * jnp.exp(jnp.minimum(gap, 0.0))).astype(BF16))
            xp = xv[rows, cols]
            both = jnp.concatenate([xp * low_lanes, xp * high_lanes], axis=0)
            inner[rows, cols] = dot(jnp.concatenate(mixing, axis=1), both)
        return 0

    lax.fori_loop(0, MIXERS // 2, inner_pair, 0)

    def in_copy(dest):
        return pltpu.make_async_remote_copy(
            src_ref=in_send.at[dest],
            dst_ref=in_recv.at[rank],
            send_sem=ins.at[dest],
            recv_sem=inr.at[rank],
            device_id=(dest, tp),
            device_id_type=MESH,
        )

    def prefix(i, before):
        @pl.when(i != rank)
        def _():
            pltpu.make_async_copy(st_recv.at[i], st_recv.at[i], str_.at[i]).wait()

        in_send[i] = before.astype(BF16)

        @pl.when(i != rank)
        def _():
            in_copy(i).start()

        tail = st_recv[i, NS:, :].astype(F32)
        return (tail[0:1] + tail[1:2]) * before + st_recv[i, :NS, :].astype(F32)

    copies[7].wait()
    ones = jnp.ones((WIDE, HD), BF16)

    def absorb(half, row_index, first):
        chunk = kv[pl.ds(SIDE * row_index, SIDE)]
        keys = chunk[:, 0].reshape(WIDE, HD)
        values = jnp.concatenate([chunk[:, 1].reshape(WIDE, HD), ones], axis=1)
        lanes = [slice(j * 128, (j + 1) * 128) for j in range(WIDE // 128)]

        def score(h):
            q = qv[half * HALF : (half + 1) * HALF, h * HD : (h + 1) * HD]
            scores = dot_t(q, keys)
            if first:
                place = iota((HALF, WIDE), 0) + (y * TOK + half * HALF)
                scores = jnp.where(iota((HALF, WIDE), 1) <= place, scores, -1e30)
            return scores

        def weigh(h, scores):
            high = scores[:, lanes[0]]
            for part in lanes[1:]:
                high = jnp.maximum(high, scores[:, part])
            new = jnp.broadcast_to(jnp.max(high, axis=1, keepdims=True), (HALF, 128))
            shrink = None
            if not first:
                old = top[h]
                new = jnp.maximum(old, new)
                shrink = jnp.exp2((old - new) * SCORE_SCALE)
            top[h] = new
            new = new * SCORE_SCALE
            weights = [jnp.exp2(scores[:, p] * SCORE_SCALE - new).astype(BF16) for p in lanes]
            return jnp.concatenate(weights, axis=1), shrink

        def add_up(h, weights, shrink):
            add = dot(weights, values)
            if not first:
                add = acc[h] * jnp.concatenate([shrink, shrink], axis=1) + add
            acc[h] = add

        scores, weights = {}, {}
        for step in range(HEADS + 2):
            if step < HEADS:
                scores[step] = score(step)
            if 0 <= step - 1 < HEADS:
                weights[step - 1] = weigh(step - 1, scores.pop(step - 1))
            if 0 <= step - 2:
                add_up(step - 2, *weights.pop(step - 2))

    def wait_row(row_index):
        for yb in range(SIDE):

            @pl.when((core == 0) | (yb != y))
            def _():
                kv_copy(SIDE * row_index + yb, rank, 0).wait_recv()

    def finish(half):
        def one(h, _):
            a = acc[h]
            att[:, pl.ds(pl.multiple_of(h * HD, HD), HD)] = (a[:, :HD] / a[:, HD:]).astype(BF16)
            return 0

        lax.fori_loop(0, HEADS, one, 0)

    def project(block):
        cols = pl.ds(pl.multiple_of(block * WIDE, WIDE), WIDE)
        return dot(att[...], wv[:, cols])

    def xs_copy(half, d):
        return pltpu.make_async_remote_copy(
            src_ref=xs.at[half, d],
            dst_ref=xr.at[half, d],
            send_sem=xss.at[half, d],
            recv_sem=xsr.at[half, d],
            device_id=(rank, partner),
            device_id_type=MESH,
        )

    def far_copy(half, way):
        return pltpu.make_async_remote_copy(
            src_ref=fs.at[half, way],
            dst_ref=fr.at[half, way],
            send_sem=fss.at[half, way],
            recv_sem=fsr.at[half, way],
            device_id=(rank, up if way == 0 else down),
            device_id_type=MESH,
        )

    def near_copy(half, way, quarter):
        return pltpu.make_async_remote_copy(
            src_ref=ns.at[half, way, quarter],
            dst_ref=nr.at[half, way, quarter],
            send_sem=nss.at[half, way, quarter],
            recv_sem=nsr.at[half, way, quarter],
            device_id=(rank, up if way == 0 else down),
            device_id_type=MESH,
        )

    near_of = (1, 3)
    STEP = 32

    def for_partner(half, d):
        xs[half, d] = project(2 * ((z + d) % SIDE) + 1 - core).astype(BF16)
        xs_copy(half, d).start()

    def for_own(half, d):
        own[half, d] = project(2 * ((z + d) % SIDE) + core)

    def near_part(half, way, quarter, with_far):
        d = near_of[way]

        def near_sum(t, _):
            at = pl.ds(pl.multiple_of(t * STEP, STEP), STEP)
            rows = pl.ds(pl.multiple_of(64 * quarter + t * STEP, STEP), STEP)
            total = own[half, d, rows, :] + xr[half, d, rows, :].astype(F32)
            if with_far:
                total = total + fr[half, way, at, :].astype(F32)
            ns[half, way, quarter, at, :] = total.astype(BF16)
            return 0

        lax.fori_loop(0, 64 // STEP, near_sum, 0)
        near_copy(half, way, quarter).start()

    def project_and_send(half):
        for_partner(half, 2)
        for_own(half, 2)
        for_partner(half, 1)
        for_partner(half, 3)
        xs_copy(half, 2).wait_recv()
        for way in range(2):

            def far_sum(t, _):
                at = pl.ds(pl.multiple_of(t * STEP, STEP), STEP)
                rows = pl.ds(pl.multiple_of(64 * way + t * STEP, STEP), STEP)
                fs[half, way, at, :] = (
                    own[half, 2, rows, :] + xr[half, 2, rows, :].astype(F32)
                ).astype(BF16)
                return 0

            lax.fori_loop(0, 64 // STEP, far_sum, 0)
            far_copy(half, way).start()
        for way in range(2):
            d = near_of[way]
            for_own(half, d)
            xs_copy(half, d).wait_recv()
            near_part(half, way, 1 - way, False)
        for_partner(half, 0)
        for_own(half, 0)

    def near(half):
        for way in range(2):
            far_copy(half, way).wait_recv()
            near_part(half, way, way, True)

    def last(half):
        xs_copy(half, 0).wait_recv()
        for quarter in range(2):
            near_copy(half, 0, quarter).wait_recv()
            near_copy(half, 1, quarter).wait_recv()

            def last_sum(t, _):
                at = pl.ds(pl.multiple_of(t * STEP, STEP), STEP)
                rows = pl.ds(pl.multiple_of(64 * quarter + t * STEP, STEP), STEP)
                total = own[half, 0, rows, :] + xr[half, 0, rows, :].astype(F32)
                total = total + nr[half, 0, quarter, at, :].astype(F32)
                total = total + nr[half, 1, quarter, at, :].astype(F32)
                mixed_v[half, rows, :] = total.astype(BF16)
                return 0

            lax.fori_loop(0, 64 // STEP, last_sum, 0)
        mixed_out(half).start()

    def mixed_out(half):
        return pltpu.make_async_copy(
            mixed_v.at[half], mixed_hbm.at[half * HALF : (half + 1) * HALF], out_sem.at[half]
        )

    absorb(0, x, True)

    def earlier_row(i, _):
        wait_row(x - i)
        absorb(0, x - i, False)
        return 0

    lax.fori_loop(1, x + 1, earlier_row, 0)
    finish(0)
    copies[8].wait()
    project_and_send(0)
    lax.fori_loop(1, RANKS, send_state, 0)
    st_recv[rank] = st_send[rank]

    absorb(1, x, True)

    @pl.when(x == 0)
    def _():
        near(0)

    def earlier_row_again(i, _):
        absorb(1, x - i, False)

        @pl.when(i == 1)
        def _():
            near(0)

        return 0

    lax.fori_loop(1, x + 1, earlier_row_again, 0)
    finish(1)
    lax.fori_loop(0, RANKS, prefix, jnp.zeros((NS, 128), F32))
    in_recv[rank] = in_send[rank]
    project_and_send(1)
    near(1)

    copies[9].wait()
    copies[10].wait()

    def entered(i, _):
        @pl.when(i != rank)
        def _():
            pltpu.make_async_copy(in_recv.at[i], in_recv.at[i], inr.at[i]).wait()

        return 0

    lax.fori_loop(0, RANKS, entered, 0)

    def gate_chunk(ci, squares):
        cols = pl.ds(pl.multiple_of(ci * 256, 256), 256)
        enter = jnp.concatenate([in_recv[2 * ci], in_recv[2 * ci + 1]], axis=1)
        second = (expx[BL - 1 : BL, cols] * enter.astype(F32) + s0buf[:, cols]).astype(BF16)
        out = []
        for b, state in enumerate((enter, second)):
            rows = slice(b * BL, (b + 1) * BL)
            value = inner[rows, cols] + expx[rows, cols] * dot(cv[rows, :], state)
            value = value + skx[0:1, cols] * xv[rows, cols].astype(F32)
            gate = gv[rows, cols].astype(F32)
            value = value * (gate / (1.0 + jnp.exp(-gate)))
            inner[rows, cols] = value
            square = value * value
            out.append(squares[b] + (square[:, :128] + square[:, 128:]))
        return tuple(out)

    zero = jnp.zeros((BL, 128), F32)
    squares = lax.fori_loop(0, FEATURES // 256, gate_chunk, (zero, zero))
    factors = [
        lax.rsqrt(jnp.sum(s, axis=1, keepdims=True) * (1.0 / FEATURES) + 1e-05) for s in squares
    ]

    def norm_chunk(ci, _):
        cols = pl.ds(pl.multiple_of(ci * 256, 256), 256)
        for b in range(2):
            rows = slice(b * BL, (b + 1) * BL)
            ssm_v[rows, cols] = (inner[rows, cols] * factors[b] * gnv[:, cols]).astype(BF16)
        return 0

    lax.fori_loop(0, FEATURES // 256, norm_chunk, 0)
    ssm_out = pltpu.make_async_copy(ssm_v, ssm_hbm, out_sem.at[2])
    ssm_out.start()

    last(0)
    last(1)

    for d in range(1, SIDE):

        @pl.when(row_needs(y, (y + d) % SIDE))
        def _():
            kv_copy(rank, rank, d - 1).wait_send()

    for xd in range(1, SIDE):

        @pl.when(xd > x)
        def _():
            kv_copy(rank, rank, 2 + xd).wait_send()

        for d in range(1, SIDE):

            @pl.when((core == 0) & (xd > x))
            def _():
                kv_copy(rank, rank, 6 + 3 * (xd - 1) + d - 1).wait_send()

    for xb in range(SIDE - 1):

        @pl.when((core == 1) & (xb < x))
        def _():
            for d in range(1, SIDE):
                kv_copy(rank, rank, 6 + 3 * xb + d - 1).wait_send()

    def states_left(d, _):
        other = (rank + d) % RANKS
        state_copy(other).wait_send()
        in_copy(other).wait_send()
        return 0

    lax.fori_loop(1, RANKS, states_left, 0)
    for half in range(2):
        for d in range(SIDE):
            xs_copy(half, d).wait_send()
        for way in range(2):
            far_copy(half, way).wait_send()
            near_copy(half, way, 0).wait_send()
            near_copy(half, way, 1).wait_send()
    ssm_out.wait()
    mixed_out(0).wait()
    mixed_out(1).wait()


def place(a, b, a_out, b_out, a_v, b_v, sem_in, sem_out):
    parts = []
    for source, stage, target in ((b, b_v, b_out), (a, a_v, a_out)):
        for part in range(2):
            rows = slice(part * HALF, (part + 1) * HALF)
            n = len(parts)
            parts.append(
                (
                    pltpu.make_async_copy(source.at[rows], stage.at[rows], sem_in.at[n]),
                    pltpu.make_async_copy(stage.at[rows], target.at[rows], sem_out.at[n]),
                )
            )
    for arrive, _ in parts:
        arrive.start()
    for arrive, leave in parts:
        arrive.wait()
        leave.start()
    for _, leave in parts:
        leave.wait()


def local(
    queries, keys, values, out_weight, ssm_input, ssm_gate, in_map, out_map, log_decay, skip, norm_gain
):
    anywhere = pl.BlockSpec(memory_space=pl.ANY)
    sem = pltpu.SemaphoreType.DMA
    scratch = [
        pltpu.VMEM((TOK, HEADS * HD), BF16),
        pltpu.VMEM((RANKS, 2, TOK, HD), BF16),
        pltpu.VMEM((HEADS * HD, 8 * WIDE), BF16),
        pltpu.VMEM((TOK, FEATURES), BF16),
        pltpu.VMEM((TOK, FEATURES), BF16),
        pltpu.VMEM((TOK, NS), BF16),
        pltpu.VMEM((TOK, NS), BF16),
        pltpu.VMEM((MIXERS, TOK), F32),
        pltpu.VMEM((1, MIXERS), F32),
        pltpu.VMEM((1, FEATURES), F32),
        pltpu.VMEM((TOK, 128), BF16),
        pltpu.VMEM((2, 128, BL), F32),
        pltpu.VMEM((2, BL, BL), F32),
        pltpu.VMEM((2, NS, BL), BF16),
        pltpu.VMEM((TOK, 128), BF16),
        pltpu.VMEM((TOK, 128), BF16),
        pltpu.VMEM((TOK, FEATURES), F32),
        pltpu.VMEM((8, FEATURES), F32),
        pltpu.VMEM((TOK, FEATURES), F32),
        pltpu.VMEM((NS, FEATURES), F32),
        pltpu.VMEM((RANKS, PIECE, 128), BF16),
        pltpu.VMEM((RANKS, PIECE, 128), BF16),
        pltpu.VMEM((RANKS, NS, 128), BF16),
        pltpu.VMEM((RANKS, NS, 128), BF16),
        pltpu.VMEM((TOK, FEATURES), BF16),
        pltpu.VMEM((HEADS, HALF, 2 * HD), F32),
        pltpu.VMEM((HEADS, HALF, 128), F32),
        pltpu.VMEM((HALF, HEADS * HD), BF16),
        pltpu.VMEM((2, SIDE, HALF, WIDE), F32),
        pltpu.VMEM((2, SIDE, HALF, WIDE), BF16),
        pltpu.VMEM((2, SIDE, HALF, WIDE), BF16),
        pltpu.VMEM((2, 2, HALF // 2, WIDE), BF16),
        pltpu.VMEM((2, 2, HALF // 2, WIDE), BF16),
        pltpu.VMEM((2, 2, 2, HALF // 2, WIDE), BF16),
        pltpu.VMEM((2, 2, 2, HALF // 2, WIDE), BF16),
        pltpu.VMEM((2, HALF, WIDE), BF16),
        sem((11,)),
        sem((16,)),
        sem((RANKS,)),
        sem((RANKS,)),
        sem((RANKS,)),
        sem((RANKS,)),
        sem((RANKS,)),
        sem((2, SIDE)),
        sem((2, SIDE)),
        sem((2, 2)),
        sem((2, 2)),
        sem((2, 2, 2)),
        sem((2, 2, 2)),
        sem((3,)),
    ]
    mixed, ssm_out = pl.pallas_call(
        kernel,
        out_shape=(
            jax.ShapeDtypeStruct((TOK, WIDE), BF16),
            jax.ShapeDtypeStruct((TOK, FEATURES), BF16),
        ),
        in_specs=[anywhere] * 11,
        out_specs=(anywhere, anywhere),
        scratch_shapes=scratch,
        compiler_params=pltpu.CompilerParams(
            collective_id=0, has_side_effects=True, vmem_limit_bytes=60 * 1024 * 1024
        ),
        cost_estimate=pl.CostEstimate(
            flops=9_000_000_000, bytes_accessed=24_000_000, transcendentals=9_000_000
        ),
    )(
        queries, keys, values, out_weight, ssm_input, ssm_gate, in_map, out_map, log_decay.T,
        skip.reshape(1, MIXERS), norm_gain.reshape(1, FEATURES),
    )
    return pl.pallas_call(
        place,
        out_shape=(
            jax.ShapeDtypeStruct((TOK, WIDE), BF16),
            jax.ShapeDtypeStruct((TOK, FEATURES), BF16),
        ),
        in_specs=[anywhere] * 2,
        out_specs=(anywhere, anywhere),
        scratch_shapes=[
            pltpu.VMEM((TOK, WIDE), BF16),
            pltpu.VMEM((TOK, FEATURES), BF16),
            sem((4,)),
            sem((4,)),
        ],
        compiler_params=pltpu.CompilerParams(vmem_limit_bytes=60 * 1024 * 1024),
    )(mixed, ssm_out)


def solution(mesh):
    in_specs = (
        P("ctx", "tp"),
        P("ctx", "tp"),
        P("ctx", "tp"),
        P("tp", None),
        P("ctx", "tp"),
        P("ctx", "tp"),
        P("ctx", "tp"),
        P("ctx", "tp"),
        P("ctx", "tp"),
        P("tp"),
        P("tp"),
    )
    out_specs = (P("ctx", "tp"), P("ctx", "tp"))
    return jax.shard_map(local, mesh=mesh, in_specs=in_specs, out_specs=out_specs, check_vma=False)
```

```python
import math

import jax
import jax.numpy as jnp
from jax import lax
from jax.experimental import pallas as pl
from jax.experimental.pallas import tpu as pltpu
from jax.sharding import PartitionSpec as P

HD = 128
HP = 64
NS = 128
BL = 128
SIDE = 4
RANKS = SIDE * SIDE
HEADS = 8
MIXERS = 32
TOK = 256
HALF = 128
WIDE = 1024
FEATURES = MIXERS * HP
PIECE = NS + 16
MESH = pl.DeviceIdType.MESH
F32 = jnp.float32
BF16 = jnp.bfloat16
SCORE_SCALE = math.log2(math.e) / math.sqrt(HD)


def dot(a, b):
    return lax.dot_general(a, b, (((1,), (0,)), ((), ())), preferred_element_type=F32)


def dot_t(a, b):
    return lax.dot_general(a, b, (((1,), (1,)), ((), ())), preferred_element_type=F32)


def iota(shape, dim):
    return lax.broadcasted_iota(jnp.int32, shape, dim)


def split3(v):
    hi = v.astype(BF16)
    rest = v - hi.astype(F32)
    mid = rest.astype(BF16)
    lo = (rest - mid.astype(F32)).astype(BF16)
    return hi, mid, lo


def lane_split(v):
    hi, mid, lo = split3(v)
    group = iota(v.shape, 1) // MIXERS
    parts = jnp.where(
        group == 0,
        hi.astype(F32),
        jnp.where(group == 1, mid.astype(F32), jnp.where(group == 2, lo.astype(F32), 0.0)),
    )
    return parts.astype(BF16)


def spread(first_head, lanes_per_head):
    return (
        iota((128, 256), 0) % MIXERS == first_head + iota((128, 256), 1) // lanes_per_head
    ).astype(F32).astype(BF16)


def kernel(
    q_hbm, k_hbm, v_hbm, w_hbm, x_hbm, g_hbm, b_hbm, c_hbm, ld_hbm, skip_hbm, gain_hbm,
    mixed_hbm, ssm_hbm,
    qv, kv, wv, xv, gv, bv, cv, ldv, skv, gnv,
    cumsplit, cum_rows, pair_maps, bt, remsplit, expsplit, expx, skx, inner, s0buf,
    st_send, st_recv, in_send, in_recv, ssm_v,
    acc, top, att, own, xs, xr, fs, fr, ns, nr, mixed_v,
    load_sem, kv_send, kv_recv, sts, str_, ins, inr, xss, xsr, fss, fsr, nss, nsr, out_sem,
):
    rank = lax.axis_index("ctx")
    tp = lax.axis_index("tp")
    x, y = rank // SIDE, rank % SIDE
    z, core = tp // 2, tp % 2
    up = 2 * ((z + 1) % SIDE) + core
    down = 2 * ((z + SIDE - 1) % SIDE) + core
    partner = 2 * z + 1 - core

    loads = [
        (k_hbm, kv.at[rank, 0]),
        (v_hbm, kv.at[rank, 1]),
        (ld_hbm, ldv),
        (skip_hbm, skv),
        (x_hbm, xv),
        (b_hbm, bv),
        (c_hbm, cv),
        (q_hbm, qv),
        (w_hbm, wv),
        (g_hbm, gv),
        (gain_hbm, gnv),
    ]
    copies = [pltpu.make_async_copy(a, b, load_sem.at[i]) for i, (a, b) in enumerate(loads)]
    for copy in copies:
        copy.start()

    barrier = pltpu.get_barrier_semaphore()

    def greet(d, _):
        pl.semaphore_signal(barrier, inc=1, device_id=((rank + d) % RANKS, tp), device_id_type=MESH)
        return 0

    lax.fori_loop(1, RANKS, greet, 0)
    for other in (partner, up, down):
        pl.semaphore_signal(barrier, inc=1, device_id=(rank, other), device_id_type=MESH)
    pl.semaphore_wait(barrier, RANKS - 1 + 3)

    def kv_copy(block, dest, sem):
        return pltpu.make_async_remote_copy(
            src_ref=kv.at[block],
            dst_ref=kv.at[block],
            send_sem=kv_send.at[sem],
            recv_sem=kv_recv.at[block],
            device_id=(dest, tp),
            device_id_type=MESH,
        )

    def row_needs(block_y, dest_y):
        return (dest_y > block_y) | ((core == 0) & (x < SIDE - 1))

    copies[0].wait()
    copies[1].wait()
    for xd in range(SIDE - 1, 0, -1):

        @pl.when(xd > x)
        def _():
            kv_copy(rank, SIDE * xd + y, 2 + xd).start()

    for d in range(1, SIDE):
        yd = (y + d) % SIDE

        @pl.when(row_needs(y, yd))
        def _():
            kv_copy(rank, SIDE * x + yd, d - 1).start()

    copies[2].wait()
    copies[3].wait()
    repeat = (iota((MIXERS, 128), 1) % MIXERS == iota((MIXERS, 128), 0)).astype(F32).astype(BF16)
    lower = (iota((BL, BL), 0) >= iota((BL, BL), 1)).astype(F32).astype(BF16)
    decays = jnp.concatenate([ldv[...]] * 4, axis=0)
    for b in range(2):
        rows = slice(b * BL, (b + 1) * BL)
        cum = [dot(lower, part) for part in split3(decays[:, rows].T)]
        cum = (cum[0] + cum[1]) + cum[2]
        cumsplit[rows, :] = lane_split(cum)
        cum_rows[b] = cum.T
        expsplit[rows, :] = lane_split(jnp.exp(cum))
        remsplit[rows, :] = lane_split(jnp.exp(cum[BL - 1 : BL] - cum))
    skips = [dot(part, repeat) for part in split3(jnp.broadcast_to(skv[...], (8, MIXERS)))]
    skip_split = lane_split((skips[0] + skips[1]) + skips[2])
    copies[4].wait()
    copies[5].wait()
    for b in range(2):
        bt[b] = bv[b * BL : (b + 1) * BL, :].astype(F32).T.astype(BF16)

    for d in range(1, SIDE):
        yb = (y + d) % SIDE

        @pl.when(row_needs(yb, y))
        def _():
            kv_copy(SIDE * x + yb, rank, 0).wait_recv()

        @pl.when(jnp.logical_not(row_needs(yb, y)))
        def _():
            kv[SIDE * x + yb, 1] = jnp.zeros((TOK, HD), BF16)

        for xd in range(SIDE - 1, 0, -1):

            @pl.when((core == 0) & (xd > x))
            def _():
                kv_copy(SIDE * x + yb, SIDE * xd + y, 6 + 3 * (xd - 1) + d - 1).start()

    for xb in range(SIDE - 2, -1, -1):

        @pl.when((core == 1) & (xb < x))
        def _():
            kv_copy(SIDE * xb + y, rank, 0).wait_recv()
            for d in range(1, SIDE):
                kv_copy(SIDE * xb + y, SIDE * x + (y + d) % SIDE, 6 + 3 * xb + d - 1).start()

    def state_chunk(ci, _):
        cols = pl.ds(pl.multiple_of(ci * 256, 256), 256)
        e = spread(4 * ci, HP)
        ex = dot(expsplit[...], e)
        expx[:, cols] = ex
        skx[:, cols] = dot(skip_split, e)
        carried = (xv[:, cols].astype(F32) * dot(remsplit[...], e)).astype(BF16)
        s0 = dot(bt[0], carried[:BL])
        s1 = dot(bt[1], carried[BL:])
        s0buf[:, cols] = s0
        d0, d1 = ex[BL - 1 : BL], ex[2 * BL - 1 :]
        end = (d1 * s0 + s1).astype(BF16)
        decay = d0 * d1
        hi = decay.astype(BF16).astype(F32)
        row = iota((16, 256), 0)
        tail = jnp.where(row == 0, hi, jnp.where(row == 1, decay - hi, 0.0)).astype(BF16)
        for u in range(2):
            st_send[2 * ci + u, :NS, :] = end[:, u * 128 : (u + 1) * 128]
            st_send[2 * ci + u, NS:, :] = tail[:, u * 128 : (u + 1) * 128]
        return 0

    lax.fori_loop(0, FEATURES // 256, state_chunk, 0, unroll=4)

    def state_copy(piece):
        return pltpu.make_async_remote_copy(
            src_ref=st_send.at[piece],
            dst_ref=st_recv.at[rank],
            send_sem=sts.at[piece],
            recv_sem=str_.at[rank],
            device_id=(piece, tp),
            device_id_type=MESH,
        )

    def send_state(d, _):
        state_copy((rank + d) % RANKS).start()
        return 0

    copies[6].wait()
    for b in range(2):
        rows = slice(b * BL, (b + 1) * BL)
        maps = dot_t(cv[rows, :], bv[rows, :])
        pair_maps[b] = jnp.where(iota((BL, BL), 0) >= iota((BL, BL), 1), maps, 0.0)
    low_lanes = (iota((BL, 128), 1) < HP).astype(F32).astype(BF16)
    high_lanes = (iota((BL, 128), 1) >= HP).astype(F32).astype(BF16)

    def inner_pair(p, _):
        cols = pl.ds(pl.multiple_of(p * 128, 128), 128)
        down_col = dot(cumsplit[...], spread(2 * p, 128))
        for b in range(2):
            rows = slice(b * BL, (b + 1) * BL)
            mixing = []
            for u in range(2):
                gap = down_col[rows, u * 128 : (u + 1) * 128] - cum_rows[b, pl.ds(2 * p + u, 1), :]
                mixing.append((pair_maps[b] * jnp.exp(jnp.minimum(gap, 0.0))).astype(BF16))
            xp = xv[rows, cols]
            both = jnp.concatenate([xp * low_lanes, xp * high_lanes], axis=0)
            inner[rows, cols] = dot(jnp.concatenate(mixing, axis=1), both)
        return 0


    def in_copy(dest):
        return pltpu.make_async_remote_copy(
            src_ref=in_send.at[dest],
            dst_ref=in_recv.at[rank],
            send_sem=ins.at[dest],
            recv_sem=inr.at[rank],
            device_id=(dest, tp),
            device_id_type=MESH,
        )

    def prefix(i, before):
        @pl.when(i != rank)
        def _():
            pltpu.make_async_copy(st_recv.at[i], st_recv.at[i], str_.at[i]).wait()

        in_send[i] = before.astype(BF16)

        @pl.when(i != rank)
        def _():
            in_copy(i).start()

        tail = st_recv[i, NS:, :].astype(F32)
        return (tail[0:1] + tail[1:2]) * before + st_recv[i, :NS, :].astype(F32)

    copies[7].wait()
    ones = jnp.ones((WIDE, HD), BF16)

    def absorb(low, count, row_index, first):
        picked = slice(low, low + count)
        chunk = kv[pl.ds(SIDE * row_index, SIDE)]
        keys = chunk[:, 0].reshape(WIDE, HD)
        values = jnp.concatenate([chunk[:, 1].reshape(WIDE, HD), ones], axis=1)
        lanes = [slice(j * 128, (j + 1) * 128) for j in range(WIDE // 128)]

        def score(h):
            q = qv[picked, h * HD : (h + 1) * HD]
            scores = dot_t(q, keys)
            if first:
                place = iota((count, WIDE), 0) + (y * TOK + low)
                scores = jnp.where(iota((count, WIDE), 1) <= place, scores, -1e30)
            return scores

        def weigh(h, scores):
            high = scores[:, lanes[0]]
            for part in lanes[1:]:
                high = jnp.maximum(high, scores[:, part])
            new = jnp.broadcast_to(jnp.max(high, axis=1, keepdims=True), (count, 128))
            shrink = None
            if not first:
                old = top[h, picked]
                new = jnp.maximum(old, new)
                shrink = jnp.exp2((old - new) * SCORE_SCALE)
            top[h, picked] = new
            new = new * SCORE_SCALE
            weights = [jnp.exp2(scores[:, p] * SCORE_SCALE - new).astype(BF16) for p in lanes]
            return jnp.concatenate(weights, axis=1), shrink

        def add_up(h, weights, shrink):
            add = dot(weights, values)
            if not first:
                add = acc[h, picked] * jnp.concatenate([shrink, shrink], axis=1) + add
            acc[h, picked] = add

        scores, weights = {}, {}
        for step in range(HEADS + 2):
            if step < HEADS:
                scores[step] = score(step)
            if 0 <= step - 1 < HEADS:
                weights[step - 1] = weigh(step - 1, scores.pop(step - 1))
            if 0 <= step - 2:
                add_up(step - 2, *weights.pop(step - 2))

    def wait_row(row_index):
        for yb in range(SIDE):

            @pl.when((core == 0) | (yb != y))
            def _():
                kv_copy(SIDE * row_index + yb, rank, 0).wait_recv()

    def finish(half):
        def one(h, _):
            a = acc[h, half * HALF : (half + 1) * HALF]
            att[:, pl.ds(pl.multiple_of(h * HD, HD), HD)] = (a[:, :HD] / a[:, HD:]).astype(BF16)
            return 0

        lax.fori_loop(0, HEADS, one, 0)

    def project(block):
        cols = pl.ds(pl.multiple_of(block * WIDE, WIDE), WIDE)
        return dot(att[...], wv[:, cols])

    def xs_copy(half, d):
        return pltpu.make_async_remote_copy(
            src_ref=xs.at[half, d],
            dst_ref=xr.at[half, d],
            send_sem=xss.at[half, d],
            recv_sem=xsr.at[half, d],
            device_id=(rank, partner),
            device_id_type=MESH,
        )

    def far_copy(half, way):
        return pltpu.make_async_remote_copy(
            src_ref=fs.at[half, way],
            dst_ref=fr.at[half, way],
            send_sem=fss.at[half, way],
            recv_sem=fsr.at[half, way],
            device_id=(rank, up if way == 0 else down),
            device_id_type=MESH,
        )

    def near_copy(half, way, quarter):
        return pltpu.make_async_remote_copy(
            src_ref=ns.at[half, way, quarter],
            dst_ref=nr.at[half, way, quarter],
            send_sem=nss.at[half, way, quarter],
            recv_sem=nsr.at[half, way, quarter],
            device_id=(rank, up if way == 0 else down),
            device_id_type=MESH,
        )

    near_of = (1, 3)
    STEP = 32

    def for_partner(half, d):
        xs[half, d] = project(2 * ((z + d) % SIDE) + 1 - core).astype(BF16)
        xs_copy(half, d).start()

    def for_own(half, d):
        own[half, d] = project(2 * ((z + d) % SIDE) + core)

    def near_part(half, way, quarter, with_far):
        d = near_of[way]

        def near_sum(t, _):
            at = pl.ds(pl.multiple_of(t * STEP, STEP), STEP)
            rows = pl.ds(pl.multiple_of(64 * quarter + t * STEP, STEP), STEP)
            total = own[half, d, rows, :] + xr[half, d, rows, :].astype(F32)
            if with_far:
                total = total + fr[half, way, at, :].astype(F32)
            ns[half, way, quarter, at, :] = total.astype(BF16)
            return 0

        lax.fori_loop(0, 64 // STEP, near_sum, 0)
        near_copy(half, way, quarter).start()

    def project_first(half):
        for_partner(half, 2)
        for_own(half, 2)
        for_partner(half, 1)
        for_partner(half, 3)
        for_own(half, 1)

    def far(half):
        xs_copy(half, 2).wait_recv()
        for way in range(2):

            def far_sum(t, _):
                at = pl.ds(pl.multiple_of(t * STEP, STEP), STEP)
                rows = pl.ds(pl.multiple_of(64 * way + t * STEP, STEP), STEP)
                fs[half, way, at, :] = (
                    own[half, 2, rows, :] + xr[half, 2, rows, :].astype(F32)
                ).astype(BF16)
                return 0

            lax.fori_loop(0, 64 // STEP, far_sum, 0)
            far_copy(half, way).start()

    def project_rest(half):
        for_own(half, 3)
        for_partner(half, 0)
        for_own(half, 0)

    def near_alone(half):
        for way in range(2):
            xs_copy(half, near_of[way]).wait_recv()
            near_part(half, way, 1 - way, False)

    def near_with_far(half):
        for way in range(2):
            far_copy(half, way).wait_recv()
            near_part(half, way, way, True)

    def last(half):
        xs_copy(half, 0).wait_recv()
        for quarter in range(2):
            near_copy(half, 0, quarter).wait_recv()
            near_copy(half, 1, quarter).wait_recv()

            def last_sum(t, _):
                at = pl.ds(pl.multiple_of(t * STEP, STEP), STEP)
                rows = pl.ds(pl.multiple_of(64 * quarter + t * STEP, STEP), STEP)
                total = own[half, 0, rows, :] + xr[half, 0, rows, :].astype(F32)
                total = total + nr[half, 0, quarter, at, :].astype(F32)
                total = total + nr[half, 1, quarter, at, :].astype(F32)
                mixed_v[half, rows, :] = total.astype(BF16)
                return 0

            lax.fori_loop(0, 64 // STEP, last_sum, 0)
        mixed_out(half).start()

    def mixed_out(half):
        return pltpu.make_async_copy(
            mixed_v.at[half], mixed_hbm.at[half * HALF : (half + 1) * HALF], out_sem.at[half]
        )

    @pl.when(x > 0)
    def _():
        absorb(0, TOK, x, True)

    def earlier_row(i, _):
        wait_row(x - i)
        absorb(0, TOK, x - i, False)
        return 0

    lax.fori_loop(1, x, earlier_row, 0)

    @pl.when(x > 0)
    def _():
        wait_row(0)

    @pl.when(x == SIDE - 1)
    def _():
        lax.fori_loop(1, RANKS, send_state, 0)

    def last_row(half):
        @pl.when(x == 0)
        def _():
            absorb(half * HALF, HALF, 0, True)

        @pl.when(x > 0)
        def _():
            absorb(half * HALF, HALF, 0, False)

        finish(half)

    last_row(0)
    copies[8].wait()
    project_first(0)
    far(0)
    project_rest(0)

    @pl.when(x < SIDE - 1)
    def _():
        lax.fori_loop(1, RANKS, send_state, 0)

    st_recv[rank] = st_send[rank]
    for way in range(2):
        far_copy(0, way).wait_send()
    near_alone(0)

    last_row(1)
    near_with_far(0)
    project_first(1)
    far(1)
    project_rest(1)
    near_alone(1)
    lax.fori_loop(0, RANKS, prefix, jnp.zeros((NS, 128), F32))
    in_recv[rank] = in_send[rank]
    lax.fori_loop(0, MIXERS // 2, inner_pair, 0, unroll=4)
    last(0)
    near_with_far(1)
    for way in range(2):
        far_copy(1, way).wait_send()

    copies[9].wait()
    copies[10].wait()

    def entered(i, _):
        @pl.when(i != rank)
        def _():
            pltpu.make_async_copy(in_recv.at[i], in_recv.at[i], inr.at[i]).wait()

        return 0

    lax.fori_loop(0, RANKS, entered, 0)

    def gate_chunk(ci, squares):
        cols = pl.ds(pl.multiple_of(ci * 256, 256), 256)
        enter = jnp.concatenate([in_recv[2 * ci], in_recv[2 * ci + 1]], axis=1)
        second = (expx[BL - 1 : BL, cols] * enter.astype(F32) + s0buf[:, cols]).astype(BF16)
        out = []
        for b, state in enumerate((enter, second)):
            rows = slice(b * BL, (b + 1) * BL)
            value = inner[rows, cols] + expx[rows, cols] * dot(cv[rows, :], state)
            value = value + skx[0:1, cols] * xv[rows, cols].astype(F32)
            gate = gv[rows, cols].astype(F32)
            value = value * (gate / (1.0 + jnp.exp(-gate)))
            inner[rows, cols] = value
            square = value * value
            out.append(squares[b] + (square[:, :128] + square[:, 128:]))
        return tuple(out)

    zero = jnp.zeros((BL, 128), F32)
    squares = lax.fori_loop(0, FEATURES // 256, gate_chunk, (zero, zero), unroll=4)
    factors = [
        lax.rsqrt(jnp.sum(s, axis=1, keepdims=True) * (1.0 / FEATURES) + 1e-05) for s in squares
    ]

    def norm_chunk(ci, _):
        cols = pl.ds(pl.multiple_of(ci * 256, 256), 256)
        for b in range(2):
            rows = slice(b * BL, (b + 1) * BL)
            ssm_v[rows, cols] = (inner[rows, cols] * factors[b] * gnv[:, cols]).astype(BF16)
        return 0

    lax.fori_loop(0, FEATURES // 256, norm_chunk, 0, unroll=4)
    ssm_out = pltpu.make_async_copy(ssm_v, ssm_hbm, out_sem.at[2])
    ssm_out.start()
    last(1)

    for d in range(1, SIDE):

        @pl.when(row_needs(y, (y + d) % SIDE))
        def _():
            kv_copy(rank, rank, d - 1).wait_send()

    for xd in range(1, SIDE):

        @pl.when(xd > x)
        def _():
            kv_copy(rank, rank, 2 + xd).wait_send()

        for d in range(1, SIDE):

            @pl.when((core == 0) & (xd > x))
            def _():
                kv_copy(rank, rank, 6 + 3 * (xd - 1) + d - 1).wait_send()

    for xb in range(SIDE - 1):

        @pl.when((core == 1) & (xb < x))
        def _():
            for d in range(1, SIDE):
                kv_copy(rank, rank, 6 + 3 * xb + d - 1).wait_send()

    def states_left(d, _):
        other = (rank + d) % RANKS
        state_copy(other).wait_send()
        in_copy(other).wait_send()
        return 0

    lax.fori_loop(1, RANKS, states_left, 0)
    for half in range(2):
        for d in range(SIDE):
            xs_copy(half, d).wait_send()
        for way in range(2):
            near_copy(half, way, 0).wait_send()
            near_copy(half, way, 1).wait_send()
    ssm_out.wait()
    mixed_out(0).wait()
    mixed_out(1).wait()


def place(a, b, a_out, b_out, a_v, b_v, sem_in, sem_out):
    parts = []
    for source, stage, target in ((b, b_v, b_out), (a, a_v, a_out)):
        for part in range(2):
            rows = slice(part * HALF, (part + 1) * HALF)
            n = len(parts)
            parts.append(
                (
                    pltpu.make_async_copy(source.at[rows], stage.at[rows], sem_in.at[n]),
                    pltpu.make_async_copy(stage.at[rows], target.at[rows], sem_out.at[n]),
                )
            )
    for arrive, _ in parts:
        arrive.start()
    for arrive, leave in parts:
        arrive.wait()
        leave.start()
    for _, leave in parts:
        leave.wait()


def local(
    queries, keys, values, out_weight, ssm_input, ssm_gate, in_map, out_map, log_decay, skip, norm_gain
):
    anywhere = pl.BlockSpec(memory_space=pl.ANY)
    sem = pltpu.SemaphoreType.DMA
    scratch = [
        pltpu.VMEM((TOK, HEADS * HD), BF16),
        pltpu.VMEM((RANKS, 2, TOK, HD), BF16),
        pltpu.VMEM((HEADS * HD, 8 * WIDE), BF16),
        pltpu.VMEM((TOK, FEATURES), BF16),
        pltpu.VMEM((TOK, FEATURES), BF16),
        pltpu.VMEM((TOK, NS), BF16),
        pltpu.VMEM((TOK, NS), BF16),
        pltpu.VMEM((MIXERS, TOK), F32),
        pltpu.VMEM((1, MIXERS), F32),
        pltpu.VMEM((1, FEATURES), F32),
        pltpu.VMEM((TOK, 128), BF16),
        pltpu.VMEM((2, 128, BL), F32),
        pltpu.VMEM((2, BL, BL), F32),
        pltpu.VMEM((2, NS, BL), BF16),
        pltpu.VMEM((TOK, 128), BF16),
        pltpu.VMEM((TOK, 128), BF16),
        pltpu.VMEM((TOK, FEATURES), F32),
        pltpu.VMEM((8, FEATURES), F32),
        pltpu.VMEM((TOK, FEATURES), F32),
        pltpu.VMEM((NS, FEATURES), F32),
        pltpu.VMEM((RANKS, PIECE, 128), BF16),
        pltpu.VMEM((RANKS, PIECE, 128), BF16),
        pltpu.VMEM((RANKS, NS, 128), BF16),
        pltpu.VMEM((RANKS, NS, 128), BF16),
        pltpu.VMEM((TOK, FEATURES), BF16),
        pltpu.VMEM((HEADS, TOK, 2 * HD), F32),
        pltpu.VMEM((HEADS, TOK, 128), F32),
        pltpu.VMEM((HALF, HEADS * HD), BF16),
        pltpu.VMEM((2, SIDE, HALF, WIDE), F32),
        pltpu.VMEM((2, SIDE, HALF, WIDE), BF16),
        pltpu.VMEM((2, SIDE, HALF, WIDE), BF16),
        pltpu.VMEM((2, 2, HALF // 2, WIDE), BF16),
        pltpu.VMEM((2, 2, HALF // 2, WIDE), BF16),
        pltpu.VMEM((2, 2, 2, HALF // 2, WIDE), BF16),
        pltpu.VMEM((2, 2, 2, HALF // 2, WIDE), BF16),
        pltpu.VMEM((2, HALF, WIDE), BF16),
        sem((11,)),
        sem((16,)),
        sem((RANKS,)),
        sem((RANKS,)),
        sem((RANKS,)),
        sem((RANKS,)),
        sem((RANKS,)),
        sem((2, SIDE)),
        sem((2, SIDE)),
        sem((2, 2)),
        sem((2, 2)),
        sem((2, 2, 2)),
        sem((2, 2, 2)),
        sem((3,)),
    ]
    mixed, ssm_out = pl.pallas_call(
        kernel,
        out_shape=(
            jax.ShapeDtypeStruct((TOK, WIDE), BF16),
            jax.ShapeDtypeStruct((TOK, FEATURES), BF16),
        ),
        in_specs=[anywhere] * 11,
        out_specs=(anywhere, anywhere),
        scratch_shapes=scratch,
        compiler_params=pltpu.CompilerParams(
            collective_id=0, has_side_effects=True, vmem_limit_bytes=60 * 1024 * 1024
        ),
        cost_estimate=pl.CostEstimate(
            flops=9_000_000_000, bytes_accessed=24_000_000, transcendentals=9_000_000
        ),
    )(
        queries, keys, values, out_weight, ssm_input, ssm_gate, in_map, out_map, log_decay.T,
        skip.reshape(1, MIXERS), norm_gain.reshape(1, FEATURES),
    )
    return pl.pallas_call(
        place,
        out_shape=(
            jax.ShapeDtypeStruct((TOK, WIDE), BF16),
            jax.ShapeDtypeStruct((TOK, FEATURES), BF16),
        ),
        in_specs=[anywhere] * 2,
        out_specs=(anywhere, anywhere),
        scratch_shapes=[
            pltpu.VMEM((TOK, WIDE), BF16),
            pltpu.VMEM((TOK, FEATURES), BF16),
            sem((4,)),
            sem((4,)),
        ],
        compiler_params=pltpu.CompilerParams(vmem_limit_bytes=60 * 1024 * 1024),
    )(mixed, ssm_out)


def solution(mesh):
    in_specs = (
        P("ctx", "tp"),
        P("ctx", "tp"),
        P("ctx", "tp"),
        P("tp", None),
        P("ctx", "tp"),
        P("ctx", "tp"),
        P("ctx", "tp"),
        P("ctx", "tp"),
        P("ctx", "tp"),
        P("tp"),
        P("tp"),
    )
    out_specs = (P("ctx", "tp"), P("ctx", "tp"))
    return jax.shard_map(local, mesh=mesh, in_specs=in_specs, out_specs=out_specs, check_vma=False)
```

```python
import math

import jax
import jax.numpy as jnp
from jax import lax
from jax.experimental import pallas as pl
from jax.experimental.pallas import tpu as pltpu
from jax.sharding import PartitionSpec as P

HD = 128
HP = 64
NS = 128
BL = 128
SIDE = 4
RANKS = SIDE * SIDE
HEADS = 8
MIXERS = 32
TOK = 256
HALF = 128
WIDE = 1024
FEATURES = MIXERS * HP
PIECE = NS + 16
MESH = pl.DeviceIdType.MESH
F32 = jnp.float32
BF16 = jnp.bfloat16
SCORE_SCALE = math.log2(math.e) / math.sqrt(HD)


def dot(a, b):
    return lax.dot_general(a, b, (((1,), (0,)), ((), ())), preferred_element_type=F32)


def dot_t(a, b):
    return lax.dot_general(a, b, (((1,), (1,)), ((), ())), preferred_element_type=F32)


def iota(shape, dim):
    return lax.broadcasted_iota(jnp.int32, shape, dim)


def split3(v):
    hi = v.astype(BF16)
    rest = v - hi.astype(F32)
    mid = rest.astype(BF16)
    lo = (rest - mid.astype(F32)).astype(BF16)
    return hi, mid, lo


def lane_split(v):
    hi, mid, lo = split3(v)
    group = iota(v.shape, 1) // MIXERS
    parts = jnp.where(
        group == 0,
        hi.astype(F32),
        jnp.where(group == 1, mid.astype(F32), jnp.where(group == 2, lo.astype(F32), 0.0)),
    )
    return parts.astype(BF16)


def spread(first_head, lanes_per_head):
    return (
        iota((128, 256), 0) % MIXERS == first_head + iota((128, 256), 1) // lanes_per_head
    ).astype(F32).astype(BF16)


def kernel(
    q_hbm, k_hbm, v_hbm, w_hbm, x_hbm, g_hbm, b_hbm, c_hbm, ld_hbm, skip_hbm, gain_hbm,
    mixed_hbm, ssm_hbm,
    qv, kv, wv, xv, gv, bv, cv, ldv, skv, gnv,
    cumsplit, cum_rows, pair_maps, bt, remsplit, expsplit, expx, skx, inner, s0buf,
    st_send, st_recv, in_send, in_recv, ssm_v,
    acc, top, att, own, xs, xr, fs, fr, ns, nr, mixed_v,
    load_sem, kv_send, kv_recv, sts, str_, ins, inr, xss, xsr, fss, fsr, nss, nsr, out_sem,
):
    rank = lax.axis_index("ctx")
    tp = lax.axis_index("tp")
    x, y = rank // SIDE, rank % SIDE
    z, core = tp // 2, tp % 2
    up = 2 * ((z + 1) % SIDE) + core
    down = 2 * ((z + SIDE - 1) % SIDE) + core
    partner = 2 * z + 1 - core

    loads = [
        (k_hbm, kv.at[rank, 0]),
        (v_hbm, kv.at[rank, 1]),
        (ld_hbm, ldv),
        (skip_hbm, skv),
        (x_hbm, xv),
        (b_hbm, bv),
        (c_hbm, cv),
        (q_hbm, qv),
        (w_hbm, wv),
        (g_hbm, gv),
        (gain_hbm, gnv),
    ]
    copies = [pltpu.make_async_copy(a, b, load_sem.at[i]) for i, (a, b) in enumerate(loads)]
    for copy in copies:
        copy.start()

    barrier = pltpu.get_barrier_semaphore()

    def greet(d, _):
        pl.semaphore_signal(barrier, inc=1, device_id=((rank + d) % RANKS, tp), device_id_type=MESH)
        return 0

    lax.fori_loop(1, RANKS, greet, 0)
    for other in (partner, up, down):
        pl.semaphore_signal(barrier, inc=1, device_id=(rank, other), device_id_type=MESH)
    pl.semaphore_wait(barrier, RANKS - 1 + 3)

    def kv_copy(block, dest, sem):
        return pltpu.make_async_remote_copy(
            src_ref=kv.at[block],
            dst_ref=kv.at[block],
            send_sem=kv_send.at[sem],
            recv_sem=kv_recv.at[block],
            device_id=(dest, tp),
            device_id_type=MESH,
        )

    def row_needs(block_y, dest_y):
        return (dest_y > block_y) | ((core == 0) & (x < SIDE - 1))

    copies[0].wait()
    copies[1].wait()
    for xd in range(SIDE - 1, 0, -1):

        @pl.when(xd > x)
        def _():
            kv_copy(rank, SIDE * xd + y, 2 + xd).start()

    for d in range(1, SIDE):
        yd = (y + d) % SIDE

        @pl.when(row_needs(y, yd))
        def _():
            kv_copy(rank, SIDE * x + yd, d - 1).start()

    copies[2].wait()
    copies[3].wait()
    repeat = (iota((MIXERS, 128), 1) % MIXERS == iota((MIXERS, 128), 0)).astype(F32).astype(BF16)
    lower = (iota((BL, BL), 0) >= iota((BL, BL), 1)).astype(F32).astype(BF16)
    decays = jnp.concatenate([ldv[...]] * 4, axis=0)
    for b in range(2):
        rows = slice(b * BL, (b + 1) * BL)
        cum = [dot(lower, part) for part in split3(decays[:, rows].T)]
        cum = (cum[0] + cum[1]) + cum[2]
        cumsplit[rows, :] = lane_split(cum)
        cum_rows[b] = cum.T
        expsplit[rows, :] = lane_split(jnp.exp(cum))
        remsplit[rows, :] = lane_split(jnp.exp(cum[BL - 1 : BL] - cum))
    skips = [dot(part, repeat) for part in split3(jnp.broadcast_to(skv[...], (8, MIXERS)))]
    skip_split = lane_split((skips[0] + skips[1]) + skips[2])
    copies[4].wait()
    copies[5].wait()
    for b in range(2):
        bt[b] = bv[b * BL : (b + 1) * BL, :].astype(F32).T.astype(BF16)

    for d in range(1, SIDE):
        yb = (y + d) % SIDE

        @pl.when(row_needs(yb, y))
        def _():
            kv_copy(SIDE * x + yb, rank, 0).wait_recv()

        @pl.when(jnp.logical_not(row_needs(yb, y)))
        def _():
            kv[SIDE * x + yb, 1] = jnp.zeros((TOK, HD), BF16)

        for xd in range(SIDE - 1, 0, -1):

            @pl.when((core == 0) & (xd > x))
            def _():
                kv_copy(SIDE * x + yb, SIDE * xd + y, 6 + 3 * (xd - 1) + d - 1).start()

    for xb in range(SIDE - 2, -1, -1):

        @pl.when((core == 1) & (xb < x))
        def _():
            kv_copy(SIDE * xb + y, rank, 0).wait_recv()
            for d in range(1, SIDE):
                kv_copy(SIDE * xb + y, SIDE * x + (y + d) % SIDE, 6 + 3 * xb + d - 1).start()

    def state_chunk(ci, _):
        cols = pl.ds(pl.multiple_of(ci * 256, 256), 256)
        e = spread(4 * ci, HP)
        ex = dot(expsplit[...], e)
        expx[:, cols] = ex
        skx[:, cols] = dot(skip_split, e)
        carried = (xv[:, cols].astype(F32) * dot(remsplit[...], e)).astype(BF16)
        s0 = dot(bt[0], carried[:BL])
        s1 = dot(bt[1], carried[BL:])
        s0buf[:, cols] = s0
        d0, d1 = ex[BL - 1 : BL], ex[2 * BL - 1 :]
        end = (d1 * s0 + s1).astype(BF16)
        decay = d0 * d1
        hi = decay.astype(BF16).astype(F32)
        row = iota((16, 256), 0)
        tail = jnp.where(row == 0, hi, jnp.where(row == 1, decay - hi, 0.0)).astype(BF16)
        for u in range(2):
            st_send[2 * ci + u, :NS, :] = end[:, u * 128 : (u + 1) * 128]
            st_send[2 * ci + u, NS:, :] = tail[:, u * 128 : (u + 1) * 128]
        return 0

    lax.fori_loop(0, FEATURES // 256, state_chunk, 0, unroll=4)

    def state_copy(piece):
        return pltpu.make_async_remote_copy(
            src_ref=st_send.at[piece],
            dst_ref=st_recv.at[rank],
            send_sem=sts.at[piece],
            recv_sem=str_.at[rank],
            device_id=(piece, tp),
            device_id_type=MESH,
        )

    def send_state(d, _):
        state_copy((rank + d) % RANKS).start()
        return 0

    copies[6].wait()
    for b in range(2):
        rows = slice(b * BL, (b + 1) * BL)
        maps = dot_t(cv[rows, :], bv[rows, :])
        pair_maps[b] = jnp.where(iota((BL, BL), 0) >= iota((BL, BL), 1), maps, 0.0)
    low_lanes = (iota((BL, 128), 1) < HP).astype(F32).astype(BF16)
    high_lanes = (iota((BL, 128), 1) >= HP).astype(F32).astype(BF16)

    def inner_pair(p, _):
        cols = pl.ds(pl.multiple_of(p * 128, 128), 128)
        down_col = dot(cumsplit[...], spread(2 * p, 128))
        for b in range(2):
            rows = slice(b * BL, (b + 1) * BL)
            mixing = []
            for u in range(2):
                gap = down_col[rows, u * 128 : (u + 1) * 128] - cum_rows[b, pl.ds(2 * p + u, 1), :]
                mixing.append((pair_maps[b] * jnp.exp(jnp.minimum(gap, 0.0))).astype(BF16))
            xp = xv[rows, cols]
            both = jnp.concatenate([xp * low_lanes, xp * high_lanes], axis=0)
            inner[rows, cols] = dot(jnp.concatenate(mixing, axis=1), both)
        return 0


    def in_copy(dest):
        return pltpu.make_async_remote_copy(
            src_ref=in_send.at[dest],
            dst_ref=in_recv.at[rank],
            send_sem=ins.at[dest],
            recv_sem=inr.at[rank],
            device_id=(dest, tp),
            device_id_type=MESH,
        )

    def prefix(i, before):
        @pl.when(i != rank)
        def _():
            pltpu.make_async_copy(st_recv.at[i], st_recv.at[i], str_.at[i]).wait()

        in_send[i] = before.astype(BF16)

        @pl.when(i != rank)
        def _():
            in_copy(i).start()

        tail = st_recv[i, NS:, :].astype(F32)
        return (tail[0:1] + tail[1:2]) * before + st_recv[i, :NS, :].astype(F32)

    copies[7].wait()
    ones = jnp.ones((WIDE, HD), BF16)

    def absorb(low, count, row_index, first):
        picked = slice(low, low + count)
        chunk = kv[pl.ds(SIDE * row_index, SIDE)]
        keys = chunk[:, 0].reshape(WIDE, HD)
        values = jnp.concatenate([chunk[:, 1].reshape(WIDE, HD), ones], axis=1)
        lanes = [slice(j * 128, (j + 1) * 128) for j in range(WIDE // 128)]

        def score(h):
            q = qv[picked, h * HD : (h + 1) * HD]
            scores = dot_t(q, keys)
            if first:
                place = iota((count, WIDE), 0) + (y * TOK + low)
                scores = jnp.where(iota((count, WIDE), 1) <= place, scores, -1e30)
            return scores

        def weigh(h, scores):
            high = scores[:, lanes[0]]
            for part in lanes[1:]:
                high = jnp.maximum(high, scores[:, part])
            new = jnp.broadcast_to(jnp.max(high, axis=1, keepdims=True), (count, 128))
            shrink = None
            if not first:
                old = top[h, picked]
                new = jnp.maximum(old, new)
                shrink = jnp.exp2((old - new) * SCORE_SCALE)
            top[h, picked] = new
            new = new * SCORE_SCALE
            weights = [jnp.exp2(scores[:, p] * SCORE_SCALE - new).astype(BF16) for p in lanes]
            return jnp.concatenate(weights, axis=1), shrink

        def add_up(h, weights, shrink):
            add = dot(weights, values)
            if not first:
                add = acc[h, picked] * jnp.concatenate([shrink, shrink], axis=1) + add
            acc[h, picked] = add

        scores, weights = {}, {}
        for step in range(HEADS + 2):
            if step < HEADS:
                scores[step] = score(step)
            if 0 <= step - 1 < HEADS:
                weights[step - 1] = weigh(step - 1, scores.pop(step - 1))
            if 0 <= step - 2:
                add_up(step - 2, *weights.pop(step - 2))

    def wait_row(row_index):
        for yb in range(SIDE):

            @pl.when((core == 0) | (yb != y))
            def _():
                kv_copy(SIDE * row_index + yb, rank, 0).wait_recv()

    def finish(half):
        def one(h, _):
            a = acc[h, half * HALF : (half + 1) * HALF]
            att[:, pl.ds(pl.multiple_of(h * HD, HD), HD)] = (a[:, :HD] / a[:, HD:]).astype(BF16)
            return 0

        lax.fori_loop(0, HEADS, one, 0)

    def project(block):
        cols = pl.ds(pl.multiple_of(block * WIDE, WIDE), WIDE)
        return dot(att[...], wv[:, cols])

    def xs_copy(half, d):
        return pltpu.make_async_remote_copy(
            src_ref=xs.at[half, d],
            dst_ref=xr.at[half, d],
            send_sem=xss.at[half, d],
            recv_sem=xsr.at[half, d],
            device_id=(rank, partner),
            device_id_type=MESH,
        )

    def far_copy(half, way):
        return pltpu.make_async_remote_copy(
            src_ref=fs.at[half, way],
            dst_ref=fr.at[half, way],
            send_sem=fss.at[half, way],
            recv_sem=fsr.at[half, way],
            device_id=(rank, up if way == 0 else down),
            device_id_type=MESH,
        )

    def near_copy(half, way, quarter):
        return pltpu.make_async_remote_copy(
            src_ref=ns.at[half, way, quarter],
            dst_ref=nr.at[half, way, quarter],
            send_sem=nss.at[half, way, quarter],
            recv_sem=nsr.at[half, way, quarter],
            device_id=(rank, up if way == 0 else down),
            device_id_type=MESH,
        )

    near_of = (1, 3)
    STEP = 32

    def for_partner(half, d):
        xs[half, d] = project(2 * ((z + d) % SIDE) + 1 - core).astype(BF16)
        xs_copy(half, d).start()

    def for_own(half, d):
        own[half, d] = project(2 * ((z + d) % SIDE) + core)

    def near_part(half, way, quarter, with_far):
        d = near_of[way]

        def near_sum(t, _):
            at = pl.ds(pl.multiple_of(t * STEP, STEP), STEP)
            rows = pl.ds(pl.multiple_of(64 * quarter + t * STEP, STEP), STEP)
            total = own[half, d, rows, :] + xr[half, d, rows, :].astype(F32)
            if with_far:
                total = total + fr[half, way, at, :].astype(F32)
            ns[half, way, quarter, at, :] = total.astype(BF16)
            return 0

        lax.fori_loop(0, 64 // STEP, near_sum, 0)
        near_copy(half, way, quarter).start()

    def project_first(half):
        for_partner(half, 2)
        for_own(half, 2)
        for_partner(half, 1)
        for_partner(half, 3)
        for_own(half, 1)

    def far(half):
        xs_copy(half, 2).wait_recv()
        for way in range(2):

            def far_sum(t, _):
                at = pl.ds(pl.multiple_of(t * STEP, STEP), STEP)
                rows = pl.ds(pl.multiple_of(64 * way + t * STEP, STEP), STEP)
                fs[half, way, at, :] = (
                    own[half, 2, rows, :] + xr[half, 2, rows, :].astype(F32)
                ).astype(BF16)
                return 0

            lax.fori_loop(0, 64 // STEP, far_sum, 0)
            far_copy(half, way).start()

    def project_rest(half):
        for_own(half, 3)
        for_partner(half, 0)
        for_own(half, 0)

    def near_alone(half):
        for way in range(2):
            xs_copy(half, near_of[way]).wait_recv()
            near_part(half, way, 1 - way, False)

    def near_with_far(half):
        for way in range(2):
            far_copy(half, way).wait_recv()
            near_part(half, way, way, True)

    def last(half):
        xs_copy(half, 0).wait_recv()
        for quarter in range(2):
            near_copy(half, 0, quarter).wait_recv()
            near_copy(half, 1, quarter).wait_recv()

            def last_sum(t, _):
                at = pl.ds(pl.multiple_of(t * STEP, STEP), STEP)
                rows = pl.ds(pl.multiple_of(64 * quarter + t * STEP, STEP), STEP)
                total = own[half, 0, rows, :] + xr[half, 0, rows, :].astype(F32)
                total = total + nr[half, 0, quarter, at, :].astype(F32)
                total = total + nr[half, 1, quarter, at, :].astype(F32)
                mixed_v[half, rows, :] = total.astype(BF16)
                return 0

            lax.fori_loop(0, 64 // STEP, last_sum, 0)
        mixed_out(half).start()

    def mixed_out(half):
        return pltpu.make_async_copy(
            mixed_v.at[half], mixed_hbm.at[half * HALF : (half + 1) * HALF], out_sem.at[half]
        )

    @pl.when(x > 0)
    def _():
        absorb(0, TOK, x, True)

    def earlier_row(i, _):
        wait_row(x - i)
        absorb(0, TOK, x - i, False)
        return 0

    split = x // 2 + 1 - x // 2 * (1 - x // (SIDE - 1))
    lax.fori_loop(1, split, earlier_row, 0)

    def last_row(half):
        @pl.when(x == 0)
        def _():
            absorb(half * HALF, HALF, 0, True)

        def one_row(i, _):
            if half == 0:
                wait_row(x - i)

                @pl.when((x == SIDE - 1) & (i == x))
                def _():
                    lax.fori_loop(1, RANKS, send_state, 0)

            absorb(half * HALF, HALF, x - i, False)
            return 0

        lax.fori_loop(split, x + 1, one_row, 0)
        finish(half)

    last_row(0)
    copies[8].wait()
    project_first(0)
    far(0)
    project_rest(0)

    @pl.when(x < SIDE - 1)
    def _():
        lax.fori_loop(1, RANKS, send_state, 0)

    st_recv[rank] = st_send[rank]
    for way in range(2):
        far_copy(0, way).wait_send()
    near_alone(0)

    last_row(1)
    near_with_far(0)
    project_first(1)
    far(1)
    project_rest(1)
    near_alone(1)
    lax.fori_loop(0, RANKS, prefix, jnp.zeros((NS, 128), F32))
    in_recv[rank] = in_send[rank]
    lax.fori_loop(0, MIXERS // 2, inner_pair, 0, unroll=4)
    last(0)
    near_with_far(1)
    for way in range(2):
        far_copy(1, way).wait_send()

    copies[9].wait()
    copies[10].wait()

    def entered(i, _):
        @pl.when(i != rank)
        def _():
            pltpu.make_async_copy(in_recv.at[i], in_recv.at[i], inr.at[i]).wait()

        return 0

    lax.fori_loop(0, RANKS, entered, 0)

    def gate_chunk(ci, squares):
        cols = pl.ds(pl.multiple_of(ci * 256, 256), 256)
        enter = jnp.concatenate([in_recv[2 * ci], in_recv[2 * ci + 1]], axis=1)
        second = (expx[BL - 1 : BL, cols] * enter.astype(F32) + s0buf[:, cols]).astype(BF16)
        out = []
        for b, state in enumerate((enter, second)):
            rows = slice(b * BL, (b + 1) * BL)
            value = inner[rows, cols] + expx[rows, cols] * dot(cv[rows, :], state)
            value = value + skx[0:1, cols] * xv[rows, cols].astype(F32)
            gate = gv[rows, cols].astype(F32)
            value = value * (gate / (1.0 + jnp.exp(-gate)))
            inner[rows, cols] = value
            square = value * value
            out.append(squares[b] + (square[:, :128] + square[:, 128:]))
        return tuple(out)

    zero = jnp.zeros((BL, 128), F32)
    squares = lax.fori_loop(0, FEATURES // 256, gate_chunk, (zero, zero), unroll=4)
    factors = [
        lax.rsqrt(jnp.sum(s, axis=1, keepdims=True) * (1.0 / FEATURES) + 1e-05) for s in squares
    ]

    def norm_chunk(ci, _):
        cols = pl.ds(pl.multiple_of(ci * 256, 256), 256)
        for b in range(2):
            rows = slice(b * BL, (b + 1) * BL)
            ssm_v[rows, cols] = (inner[rows, cols] * factors[b] * gnv[:, cols]).astype(BF16)
        return 0

    lax.fori_loop(0, FEATURES // 256, norm_chunk, 0, unroll=4)
    ssm_out = pltpu.make_async_copy(ssm_v, ssm_hbm, out_sem.at[2])
    ssm_out.start()
    last(1)

    for d in range(1, SIDE):

        @pl.when(row_needs(y, (y + d) % SIDE))
        def _():
            kv_copy(rank, rank, d - 1).wait_send()

    for xd in range(1, SIDE):

        @pl.when(xd > x)
        def _():
            kv_copy(rank, rank, 2 + xd).wait_send()

        for d in range(1, SIDE):

            @pl.when((core == 0) & (xd > x))
            def _():
                kv_copy(rank, rank, 6 + 3 * (xd - 1) + d - 1).wait_send()

    for xb in range(SIDE - 1):

        @pl.when((core == 1) & (xb < x))
        def _():
            for d in range(1, SIDE):
                kv_copy(rank, rank, 6 + 3 * xb + d - 1).wait_send()

    def states_left(d, _):
        other = (rank + d) % RANKS
        state_copy(other).wait_send()
        in_copy(other).wait_send()
        return 0

    lax.fori_loop(1, RANKS, states_left, 0)
    for half in range(2):
        for d in range(SIDE):
            xs_copy(half, d).wait_send()
        for way in range(2):
            near_copy(half, way, 0).wait_send()
            near_copy(half, way, 1).wait_send()
    ssm_out.wait()
    mixed_out(0).wait()
    mixed_out(1).wait()


def place(a, b, a_out, b_out, a_v, b_v, sem_in, sem_out):
    parts = []
    for source, stage, target in ((b, b_v, b_out), (a, a_v, a_out)):
        for part in range(2):
            rows = slice(part * HALF, (part + 1) * HALF)
            n = len(parts)
            parts.append(
                (
                    pltpu.make_async_copy(source.at[rows], stage.at[rows], sem_in.at[n]),
                    pltpu.make_async_copy(stage.at[rows], target.at[rows], sem_out.at[n]),
                )
            )
    for arrive, _ in parts:
        arrive.start()
    for arrive, leave in parts:
        arrive.wait()
        leave.start()
    for _, leave in parts:
        leave.wait()


def local(
    queries, keys, values, out_weight, ssm_input, ssm_gate, in_map, out_map, log_decay, skip, norm_gain
):
    anywhere = pl.BlockSpec(memory_space=pl.ANY)
    sem = pltpu.SemaphoreType.DMA
    scratch = [
        pltpu.VMEM((TOK, HEADS * HD), BF16),
        pltpu.VMEM((RANKS, 2, TOK, HD), BF16),
        pltpu.VMEM((HEADS * HD, 8 * WIDE), BF16),
        pltpu.VMEM((TOK, FEATURES), BF16),
        pltpu.VMEM((TOK, FEATURES), BF16),
        pltpu.VMEM((TOK, NS), BF16),
        pltpu.VMEM((TOK, NS), BF16),
        pltpu.VMEM((MIXERS, TOK), F32),
        pltpu.VMEM((1, MIXERS), F32),
        pltpu.VMEM((1, FEATURES), F32),
        pltpu.VMEM((TOK, 128), BF16),
        pltpu.VMEM((2, 128, BL), F32),
        pltpu.VMEM((2, BL, BL), F32),
        pltpu.VMEM((2, NS, BL), BF16),
        pltpu.VMEM((TOK, 128), BF16),
        pltpu.VMEM((TOK, 128), BF16),
        pltpu.VMEM((TOK, FEATURES), F32),
        pltpu.VMEM((8, FEATURES), F32),
        pltpu.VMEM((TOK, FEATURES), F32),
        pltpu.VMEM((NS, FEATURES), F32),
        pltpu.VMEM((RANKS, PIECE, 128), BF16),
        pltpu.VMEM((RANKS, PIECE, 128), BF16),
        pltpu.VMEM((RANKS, NS, 128), BF16),
        pltpu.VMEM((RANKS, NS, 128), BF16),
        pltpu.VMEM((TOK, FEATURES), BF16),
        pltpu.VMEM((HEADS, TOK, 2 * HD), F32),
        pltpu.VMEM((HEADS, TOK, 128), F32),
        pltpu.VMEM((HALF, HEADS * HD), BF16),
        pltpu.VMEM((2, SIDE, HALF, WIDE), F32),
        pltpu.VMEM((2, SIDE, HALF, WIDE), BF16),
        pltpu.VMEM((2, SIDE, HALF, WIDE), BF16),
        pltpu.VMEM((2, 2, HALF // 2, WIDE), BF16),
        pltpu.VMEM((2, 2, HALF // 2, WIDE), BF16),
        pltpu.VMEM((2, 2, 2, HALF // 2, WIDE), BF16),
        pltpu.VMEM((2, 2, 2, HALF // 2, WIDE), BF16),
        pltpu.VMEM((2, HALF, WIDE), BF16),
        sem((11,)),
        sem((16,)),
        sem((RANKS,)),
        sem((RANKS,)),
        sem((RANKS,)),
        sem((RANKS,)),
        sem((RANKS,)),
        sem((2, SIDE)),
        sem((2, SIDE)),
        sem((2, 2)),
        sem((2, 2)),
        sem((2, 2, 2)),
        sem((2, 2, 2)),
        sem((3,)),
    ]
    mixed, ssm_out = pl.pallas_call(
        kernel,
        out_shape=(
            jax.ShapeDtypeStruct((TOK, WIDE), BF16),
            jax.ShapeDtypeStruct((TOK, FEATURES), BF16),
        ),
        in_specs=[anywhere] * 11,
        out_specs=(anywhere, anywhere),
        scratch_shapes=scratch,
        compiler_params=pltpu.CompilerParams(
            collective_id=0, has_side_effects=True, vmem_limit_bytes=60 * 1024 * 1024
        ),
        cost_estimate=pl.CostEstimate(
            flops=9_000_000_000, bytes_accessed=24_000_000, transcendentals=9_000_000
        ),
    )(
        queries, keys, values, out_weight, ssm_input, ssm_gate, in_map, out_map, log_decay.T,
        skip.reshape(1, MIXERS), norm_gain.reshape(1, FEATURES),
    )
    return pl.pallas_call(
        place,
        out_shape=(
            jax.ShapeDtypeStruct((TOK, WIDE), BF16),
            jax.ShapeDtypeStruct((TOK, FEATURES), BF16),
        ),
        in_specs=[anywhere] * 2,
        out_specs=(anywhere, anywhere),
        scratch_shapes=[
            pltpu.VMEM((TOK, WIDE), BF16),
            pltpu.VMEM((TOK, FEATURES), BF16),
            sem((4,)),
            sem((4,)),
        ],
        compiler_params=pltpu.CompilerParams(vmem_limit_bytes=60 * 1024 * 1024),
    )(mixed, ssm_out)


def solution(mesh):
    in_specs = (
        P("ctx", "tp"),
        P("ctx", "tp"),
        P("ctx", "tp"),
        P("tp", None),
        P("ctx", "tp"),
        P("ctx", "tp"),
        P("ctx", "tp"),
        P("ctx", "tp"),
        P("ctx", "tp"),
        P("tp"),
        P("tp"),
    )
    out_specs = (P("ctx", "tp"), P("ctx", "tp"))
    return jax.shard_map(local, mesh=mesh, in_specs=in_specs, out_specs=out_specs, check_vma=False)
```
